1024 devices in a mesh: gx: 64 (over y, x), gy: 16 (over z, core).
Axes of the slice: x: 8, y: 8, z: 8, core: 2. Of those that a mesh axis runs over, the one named last changes fastest.
Arguments:
- water_depth: float32 [512, 16384], P('gx', 'gy'), may hold values from 0 to 2
- velocity: float32 [2, 512, 16384], P(None, 'gx', 'gy'), may hold values from -1.2 to 1.2
- bathymetry: float32 [512, 16384], P('gx', 'gy'), may hold values from -0.5 to 0.5
- wet_tiles: int32 [64, 128], P('gx', 'gy'), may hold values from 0 to 1, as said below
- migration: int32 [64, 128], P('gx', 'gy'), may hold values from 0 to 15, as said below
Outputs:
- final_state: float32 [3, 512, 16384], P(None, 'gx', 'gy')
The draws below stay inside these ranges and needn't reach their ends.
Inputs may be any that keep to these rules, and one draw needn't show every extreme that they name: `wet_tiles`: after the tiles move, every device holds exactly 4 wet tiles. `migration`: the 8 tiles of one device go to distinct devices of its row of tiles (itself possibly among them), and every device receives exactly one tile for each value of t mod 8.
All inputs are finite; a program needn't handle non-finite values.
Results may differ from the reference program's by a relative error of at most 0.0003.
Values sent between devices are 32-bit elements; how exact they have to be, the bound alone decides.
A program may use at most 32 MiB of HBM per device.

```python
import jax
import jax.numpy as jnp
from jax import lax

TILE_R = 8
TILE_C = 128
STEPS = 4
HALO = 4
TILES_DEV = 8
ROWS = 512
TILE_COLS = 128
COLS = 16384


def plan_rows(key):
    band_count = ROWS // TILE_R
    group_size = TILE_COLS // TILES_DEV
    row_keys = jax.random.split(key, band_count)

    def one_row(row_key):
        key_order, key_shift, key_rank = jax.random.split(row_key, 3)
        ordering = jax.random.permutation(key_order, group_size).astype(jnp.int32)
        inverse = jnp.zeros((group_size,), jnp.int32).at[ordering].set(jnp.arange(group_size, dtype=jnp.int32))
        shifts = jax.random.permutation(key_shift, group_size).astype(jnp.int32)[:TILES_DEV]
        destination = inverse[(ordering[:, None] + shifts[None, :]) % group_size]
        rankings = jax.vmap(lambda small_key: jax.random.permutation(small_key, TILES_DEV).astype(jnp.int32))(jax.random.split(key_rank, group_size))
        wetness = (rankings[destination, jnp.arange(TILES_DEV, dtype=jnp.int32)[None, :]] < TILES_DEV // 2).astype(jnp.int32)
        return (destination.reshape(-1), wetness.reshape(-1))
    return jax.vmap(one_row)(row_keys)


def draw_wet_tiles(key, part):
    return plan_rows(key)[1].astype(jnp.int32)


def draw_migration(key, part):
    return plan_rows(key)[0].astype(jnp.int32)


def levels(own_key, dims, shards, low, top_value):
    factor_of, own = 1.0, jax.random.fold_in(own_key, 6)
    for position, blocks in shards:
        heights = jnp.exp(jax.random.uniform(jax.random.fold_in(own, position), (blocks,), jnp.float32, low / len(shards), top_value / len(shards)))
        factor_of = factor_of * jnp.repeat(heights, dims[position] // blocks).reshape([-1 if axis == position else 1 for axis in range(len(dims))])
    return factor_of


def normal_values(rng, shape, spread, bound, cuts=(), held_as=jnp.bfloat16):
    level = levels(rng, shape, cuts, -0.22, 0.18) if cuts else 1.0
    entries = jax.random.normal(rng, shape, jnp.float32) * spread * level
    return jnp.minimum(jnp.maximum(entries, -bound), bound).astype(held_as)


def setup_inputs(seed: int = 0) -> dict:
    splits = jax.random.split(jax.random.key(seed), 6)
    return {
        "water_depth": jnp.clip(2.0 * jax.random.uniform(splits[0], (ROWS, COLS), jnp.float32) ** levels(splits[0], (ROWS, COLS), ((0, 64), (1, 16)), -0.2, 0.2), 0.0, 2.0),
        "velocity": normal_values(splits[1], (2, ROWS, COLS), 0.3, 1.2, ((1, 64), (2, 16)), jnp.float32),
        "bathymetry": jnp.clip(jax.random.uniform(splits[2], (ROWS, COLS), jnp.float32, -0.5, 0.5) * levels(splits[2], (ROWS, COLS), ((0, 64), (1, 16)), -0.4, 0.0), -0.5, 0.5),
        "wet_tiles": draw_wet_tiles(jax.random.fold_in(splits[5], 71), 0),
        "migration": draw_migration(jax.random.fold_in(splits[5], 71), 0),
    }


GRAVITY = 1.0
DRY_DEPTH = 0.05
COURANT = 0.15

def fluxes(current, bedrock):
    water = current[0]
    momentum_x = current[1]
    momentum_y = current[2]
    floored = jnp.maximum(water, DRY_DEPTH)
    velocity_x = momentum_x / floored
    velocity_y = momentum_y / floored
    celerity = jnp.sqrt(GRAVITY * floored)
    pressure = 0.5 * GRAVITY * water * water
    flux_east = jnp.stack([momentum_x, momentum_x * velocity_x + pressure, momentum_y * velocity_x])
    flux_north = jnp.stack([momentum_y, momentum_x * velocity_y, momentum_y * velocity_y + pressure])
    reach_east = jnp.abs(velocity_x) + celerity
    reach_north = jnp.abs(velocity_y) + celerity
    wave_east = jnp.maximum(reach_east[:, 1:], reach_east[:, :-1])
    wave_north = jnp.maximum(reach_north[1:], reach_north[:-1])
    face_east = 0.5 * (flux_east[:, :, 1:] + flux_east[:, :, :-1]) - 0.5 * wave_east * (current[:, :, 1:] - current[:, :, :-1])
    face_north = 0.5 * (flux_north[:, 1:] + flux_north[:, :-1]) - 0.5 * wave_north * (current[:, 1:] - current[:, :-1])
    spread_east = face_east[:, 1:-1, 1:] - face_east[:, 1:-1, :-1]
    spread_north = face_north[:, 1:, 1:-1] - face_north[:, :-1, 1:-1]
    interior = water[1:-1, 1:-1]
    slope_east = 0.5 * (bedrock[1:-1, 2:] - bedrock[1:-1, :-2])
    slope_north = 0.5 * (bedrock[2:, 1:-1] - bedrock[:-2, 1:-1])
    sources = jnp.stack([jnp.zeros_like(interior), -GRAVITY * interior * slope_east, -GRAVITY * interior * slope_north])
    return sources - spread_east - spread_north

def inside(extent, row_start, col_start, rows_total, cols_total):
    grid_rows = row_start + lax.broadcasted_iota(jnp.int32, extent, 0)
    grid_cols = col_start + lax.broadcasted_iota(jnp.int32, extent, 1)
    inside_grid = (grid_rows >= 0) & (grid_rows < rows_total) & (grid_cols >= 0) & (grid_cols < cols_total)
    return inside_grid.astype(jnp.float32)

def advance(padded, row_start, col_start, rows_total, cols_total):
    current = padded[:3]
    bedrock = padded[3]
    offset = 0
    for substep in range(2):
        section_one = current[:, 1:-1, 1:-1] + COURANT * fluxes(current, bedrock)
        section_one = section_one * inside(section_one.shape[1:], row_start + offset + 1, col_start + offset + 1, rows_total, cols_total)
        section_two = 0.5 * current[:, 2:-2, 2:-2] + 0.5 * (section_one[:, 1:-1, 1:-1] + COURANT * fluxes(section_one, bedrock[1:-1, 1:-1]))
        offset = offset + 2
        section_two = section_two * inside(section_two.shape[1:], row_start + offset, col_start + offset, rows_total, cols_total)
        current = section_two
        bedrock = bedrock[2:-2, 2:-2]
    return current

def reference(water_depth, velocity, bathymetry, wet_tiles, migration):
    rows_total = water_depth.shape[0]
    cols_total = water_depth.shape[1]
    band_count = rows_total // TILE_R
    current = jnp.stack([water_depth, water_depth * velocity[0], water_depth * velocity[1]])
    wet_cells = jnp.repeat(wet_tiles, TILE_C, axis=1)
    for period in range(STEPS // 2):
        fields = jnp.concatenate([current, bathymetry[None]], axis=0)
        padded = jnp.pad(fields, ((0, 0), (HALO, HALO), (HALO, HALO)))

        def one_band(band_index):
            band_start = band_index * TILE_R
            band_fields = lax.dynamic_slice_in_dim(padded, band_start, TILE_R + 2 * HALO, 1)
            advanced = advance(band_fields, band_start - HALO, -HALO, rows_total, cols_total)
            previous = lax.dynamic_slice_in_dim(current, band_start, TILE_R, 1)
            wet_row = lax.dynamic_index_in_dim(wet_cells, band_index, 0, keepdims=False)
            return jnp.where(wet_row[None, None, :] > 0, advanced, previous)
        band_results = lax.map(one_band, jnp.arange(band_count, dtype=jnp.int32))
        current = jnp.transpose(band_results, (1, 0, 2, 3)).reshape(3, rows_total, cols_total)
    tile_cols = cols_total // TILE_C
    local_index = jnp.arange(tile_cols, dtype=jnp.int32) % TILES_DEV
    target = (migration * TILES_DEV + local_index[None, :]).astype(jnp.int32)
    band_ids = jnp.arange(band_count, dtype=jnp.int32)[:, None] + jnp.zeros_like(target)
    source = jnp.zeros_like(target).at[band_ids, target].set(jnp.arange(tile_cols, dtype=jnp.int32)[None, :] + jnp.zeros_like(target))
    tile_view = current.reshape(3, band_count, TILE_R, tile_cols, TILE_C)
    placed = jnp.take_along_axis(tile_view, source[None, :, None, :, None], axis=3)
    return placed.reshape(3, rows_total, cols_total)
```

```python
import functools

import jax
import jax.numpy as jnp
from jax import lax
from jax.experimental import pallas as pl
from jax.experimental.pallas import tpu as pltpu
from jax.sharding import PartitionSpec as P

DRY_DEPTH = 0.05
COURANT = 0.15
HALO = 4
ROWS = 8
LANES = 128
REACH = 8
WET_LANE = 32
MESH = pl.DeviceIdType.MESH
CORNERS = ((0, 0), (1, 0), (0, 1), (1, 1))


def lanes_of(shape):
    return lax.broadcasted_iota(jnp.int32, shape, len(shape) - 1)


def turn(x, by, axis):
    return pltpu.roll(x, by % x.shape[axis], axis)


def ring_next(tiles):
    turned = [turn(x, -1, 1) for x in tiles]
    last = lanes_of(turned[0].shape) == LANES - 1
    return [jnp.where(last, turned[(c + 1) % len(tiles)], turned[c]) for c in range(len(tiles))]


def ring_previous(tiles):
    turned = [turn(x, 1, 1) for x in tiles]
    first = lanes_of(turned[0].shape) == 0
    return [jnp.where(first, turned[c - 1], turned[c]) for c in range(len(tiles))]


def rates(state):
    parts = []
    for h, p, q in state:
        floored = jnp.maximum(h, DRY_DEPTH)
        inverse_root = lax.rsqrt(floored)
        celerity = floored * inverse_root
        inverse = inverse_root * inverse_root
        u = p * inverse
        v = q * inverse
        pressure = 0.5 * h * h
        parts.append(
            (h, p, q, p * u + pressure, q * u, q * v + pressure, jnp.abs(u) + celerity, jnp.abs(v) + celerity)
        )
    fields = list(zip(*parts))
    h, p, q, east, cross, north, reach_x, reach_y = fields
    on = [ring_next(x) for x in (h, p, q, east, cross, reach_x)]
    faces = [[], [], []]
    for c in range(len(state)):
        wave = jnp.maximum(reach_x[c], on[5][c])
        faces[0].append(p[c] + on[1][c] - wave * (on[0][c] - h[c]))
        faces[1].append(east[c] + on[3][c] - wave * (on[1][c] - p[c]))
        faces[2].append(cross[c] + on[4][c] - wave * (on[2][c] - q[c]))
    back = [ring_previous(x) for x in faces]
    out = []
    for c in range(len(state)):
        below = [turn(x[c], -1, 0) for x in (h, p, q, cross, north, reach_y)]
        wave = jnp.maximum(reach_y[c], below[5])
        rows = (
            q[c] + below[2] - wave * (below[0] - h[c]),
            cross[c] + below[3] - wave * (below[1] - p[c]),
            north[c] + below[4] - wave * (below[2] - q[c]),
        )
        out.append(
            tuple((faces[f][c] - back[f][c]) + (rows[f] - turn(rows[f], 1, 0)) for f in range(3))
        )
    return out


def half_step(state, slopes, masks, start):
    out = []
    changes = rates(state)
    for c, (cells, change, slope, mask) in enumerate(zip(state, changes, slopes, masks)):
        moved = [cells[0] - (0.5 * COURANT) * change[0]]
        for f in (1, 2):
            moved.append(cells[f] - (0.5 * COURANT) * change[f] - cells[0] * slope[f - 1])
        if start is not None:
            moved = [0.5 * start[c][f] + 0.5 * moved[f] for f in range(3)]
        out.append(tuple(x * mask for x in moved))
    return out


def two_steps(state, slopes, masks):
    for _ in range(2):
        middle = half_step(state, slopes, masks, None)
        state = half_step(middle, slopes, masks, state)
    return state


def kernel(
    sizes,
    depth_hbm,
    velocity_hbm,
    bed_hbm,
    wet_hbm,
    migration_hbm,
    out_ref,
    own,
    above,
    below,
    strip,
    strips,
    corners,
    wet,
    migration,
    homes,
    homes_flat,
    tiles,
    outgoing,
    arrived,
    load_sem,
    flat_sem,
    halo_send,
    halo_recv,
    strip_send,
    strip_recv,
    corner_send,
    corner_recv,
    home_send,
    home_recv,
    slot_send,
    slot_recv,
):
    n_rows, n_cols = sizes
    tile_count = own.shape[2] // LANES
    gx, gy = lax.axis_index("gx"), lax.axis_index("gy")
    up, down = lax.rem(gx + n_rows - 1, n_rows), lax.rem(gx + 1, n_rows)
    left, right = lax.rem(gy + n_cols - 1, n_cols), lax.rem(gy + 1, n_cols)
    corner_ids = [((up, down)[r], (left, right)[s]) for r, s in CORNERS]

    def row_mate(k):
        return (gx, lax.rem(gy + k, n_cols))

    barrier = pltpu.get_barrier_semaphore()
    friends = [row_mate(k) for k in range(1, n_cols)] + [(up, gy), (down, gy)] + corner_ids
    for friend in friends:
        pl.semaphore_signal(barrier, inc=1, device_id=friend, device_id_type=MESH)

    loads = [
        pltpu.make_async_copy(wet_hbm, wet, load_sem.at[0]),
        pltpu.make_async_copy(migration_hbm, migration, load_sem.at[1]),
        pltpu.make_async_copy(migration_hbm, homes.at[0], load_sem.at[2]),
        pltpu.make_async_copy(depth_hbm, own.at[0], load_sem.at[3]),
        pltpu.make_async_copy(velocity_hbm, own.at[pl.ds(1, 2)], load_sem.at[4]),
        pltpu.make_async_copy(bed_hbm, own.at[3], load_sem.at[5]),
    ]
    for load in loads:
        load.start()
    for load in loads:
        load.wait()

    lane = lanes_of((ROWS, LANES))
    packed = jnp.zeros((ROWS, LANES), jnp.float32)
    for f in range(4):
        first, last = own[f, :, 0:LANES], own[f, :, (tile_count - 1) * LANES : tile_count * LANES]
        at = REACH * f
        packed = jnp.where((lane >= at) & (lane < at + REACH), turn(first, at, 1) if f else first, packed)
        at = LANES - REACH * (f + 1)
        packed = jnp.where((lane >= at) & (lane < at + REACH), turn(last, -REACH * f, 1) if f else last, packed)
    for t in range(tile_count):
        packed = jnp.where(lane == WET_LANE + t, wet[0, t].astype(jnp.float32), packed)
    strip[...] = packed

    pl.semaphore_wait(barrier, len(friends))

    def remote(source, target, send, receive, where):
        return pltpu.make_async_remote_copy(
            src_ref=source, dst_ref=target, send_sem=send, recv_sem=receive, device_id=where, device_id_type=MESH
        )

    halos = [
        remote(own, below, halo_send.at[0], halo_recv.at[0], (up, gy)),
        remote(own, above, halo_send.at[1], halo_recv.at[1], (down, gy)),
    ]
    places = [(up, gy), (down, gy), (gx, left), (gx, right)]
    sides = [
        remote(strip, strips.at[i], strip_send.at[i], strip_recv.at[i], where) for i, where in enumerate(places)
    ]
    diagonals = [
        remote(strip, corners.at[i], corner_send.at[i], corner_recv.at[i], where)
        for i, where in enumerate(corner_ids)
    ]
    mates = [
        remote(homes.at[0], homes.at[k], home_send.at[k], home_recv.at[k], row_mate(k)) for k in range(1, n_cols)
    ]
    for copy in sides + diagonals + halos + mates:
        copy.start()

    chosen = []
    for k in range(n_cols):
        target = row_mate(k)[1]
        index = jnp.int32(0)
        for t in range(1, tile_count):
            index = jnp.where(migration[0, t] == target, t, index)
        chosen.append(index)

    for copy in sides + diagonals + halos:
        copy.wait_recv()

    def columns(reference, f):
        return [reference[f, :, c * LANES : (c + 1) * LANES] for c in range(tile_count)]

    def ends(from_left, from_right, f):
        head = turn(from_right, -REACH * f, 1) if f else from_right
        tail = turn(from_left, REACH * f, 1) if f else from_left
        return jnp.where(lane < REACH, head, jnp.where(lane >= LANES - REACH, tail, 0.0))

    lower_right, upper_right, lower_left, upper_left = (corners[i] for i in range(4))
    bands = (
        (above, upper_left, upper_right, strips[1]),
        (own, strips[3], strips[2], strip[...]),
        (below, lower_left, lower_right, strips[0]),
    )
    fields = []
    for f in range(4):
        stacked = [columns(band[0], f) + [ends(band[1], band[2], f)] for band in bands]
        fields.append([jnp.concatenate([s[c] for s in stacked], axis=0) for c in range(tile_count + 1)])

    def spread(tile, at):
        return jnp.broadcast_to(tile[:, at : at + 1], (ROWS, LANES))

    wets = []
    for c in range(tile_count + 1):
        stacked = []
        for _, from_left, from_right, flags in bands:
            if c < tile_count:
                stacked.append(spread(flags, WET_LANE + c))
            else:
                stacked.append(
                    jnp.where(
                        lane < LANES // 2, spread(from_right, WET_LANE), spread(from_left, WET_LANE + tile_count - 1)
                    )
                )
        wets.append(jnp.concatenate(stacked, axis=0))

    row = lax.broadcasted_iota(jnp.int32, (3 * ROWS, LANES), 0)
    wide = lanes_of((3 * ROWS, LANES))
    one, zero = jnp.float32(1), jnp.float32(0)
    has_up, has_down = jnp.where(gx > 0, one, zero), jnp.where(gx < n_rows - 1, one, zero)
    has_left, has_right = jnp.where(gy > 0, one, zero), jnp.where(gy < n_cols - 1, one, zero)
    inside_rows = jnp.where(row < ROWS, has_up, jnp.where(row >= 2 * ROWS, has_down, one))
    inside_ends = inside_rows * jnp.where(wide < LANES // 2, has_right, has_left)
    masks = [inside_rows] * tile_count + [inside_ends]

    depth, across, along, bed = fields
    state = []
    beds = []
    for c in range(tile_count + 1):
        h = depth[c] * masks[c]
        state.append((h, h * across[c], h * along[c]))
        beds.append(bed[c] * masks[c])
    bed_next, bed_previous = ring_next(beds), ring_previous(beds)
    slopes = [
        (
            (0.5 * COURANT) * (bed_next[c] - bed_previous[c]),
            (0.5 * COURANT) * (turn(beds[c], -1, 0) - turn(beds[c], 1, 0)),
        )
        for c in range(tile_count + 1)
    ]
    advanced = two_steps(state, slopes, masks)
    state = [
        tuple(jnp.where(w > 0.5, new, old) for new, old in zip(a, s)) for w, a, s in zip(wets, advanced, state)
    ]

    def narrow(x, start, size):
        return turn(x, -start, 0)[:size]

    kept = 2 * HALO + ROWS
    state = [tuple(narrow(x, ROWS - HALO, kept) for x in s) for s in state]
    slopes = [tuple(narrow(x, ROWS - HALO, kept) for x in s) for s in slopes]
    masks = [narrow(x, ROWS - HALO, kept) for x in masks]
    advanced = two_steps(state, slopes, masks)
    for t in range(tile_count):
        for f in range(3):
            new, old = narrow(advanced[t][f], HALO, ROWS), narrow(state[t][f], HALO, ROWS)
            tiles[t, f] = jnp.where(wets[t][ROWS : 2 * ROWS] > 0.5, new, old)

    slots = []
    for k in sorted(range(1, n_cols), key=lambda k: -min(k, n_cols - k)):
        outgoing[k] = tiles[chosen[k]]
        copy = remote(outgoing.at[k], arrived.at[k], slot_send.at[k], slot_recv.at[k], row_mate(k))
        copy.start()
        slots.append(copy)
    arrived[0] = tiles[chosen[0]]

    for copy in mates:
        copy.wait_recv()
    flat = pltpu.make_async_copy(homes, homes_flat, flat_sem.at[0])
    flat.start()
    flat.wait()
    sources = []
    for t in range(tile_count):
        index = jnp.int32(0)
        for k in range(1, n_cols):
            index = jnp.where(homes_flat[k, 0, t] == gy, k, index)
        sources.append(index)
    for copy in slots:
        copy.wait_recv()
    for t in range(tile_count):
        out_ref[:, :, t * LANES : (t + 1) * LANES] = arrived[sources[t]]
    for copy in sides + diagonals + halos + mates + slots:
        copy.wait_send()


def solution(mesh):
    n_rows, n_cols = mesh.shape["gx"], mesh.shape["gy"]

    def step(water_depth, velocity, bathymetry, wet_tiles, migration):
        rows, cols = water_depth.shape
        tile_count = wet_tiles.shape[1]
        block = (4, rows, cols)
        dma = pltpu.SemaphoreType.DMA
        return pl.pallas_call(
            functools.partial(kernel, (n_rows, n_cols)),
            out_shape=jax.ShapeDtypeStruct((3, rows, cols), jnp.float32),
            in_specs=[pl.BlockSpec(memory_space=pl.ANY)] * 5,
            out_specs=pl.BlockSpec(memory_space=pltpu.VMEM),
            scratch_shapes=[
                pltpu.VMEM(block, jnp.float32),
                pltpu.VMEM(block, jnp.float32),
                pltpu.VMEM(block, jnp.float32),
                pltpu.VMEM((ROWS, LANES), jnp.float32),
                pltpu.VMEM((4, ROWS, LANES), jnp.float32),
                pltpu.VMEM((4, ROWS, LANES), jnp.float32),
                pltpu.SMEM((1, tile_count), jnp.int32),
                pltpu.SMEM((1, tile_count), jnp.int32),
                pltpu.VMEM((n_cols, 1, tile_count), jnp.int32),
                pltpu.SMEM((n_cols, 1, tile_count), jnp.int32),
                pltpu.VMEM((tile_count, 3, rows, LANES), jnp.float32),
                pltpu.VMEM((n_cols, 3, rows, LANES), jnp.float32),
                pltpu.VMEM((n_cols, 3, rows, LANES), jnp.float32),
                dma((6,)),
                dma((1,)),
                dma((2,)),
                dma((2,)),
                dma((4,)),
                dma((4,)),
                dma((4,)),
                dma((4,)),
                dma((n_cols,)),
                dma((n_cols,)),
                dma((n_cols,)),
                dma((n_cols,)),
            ],
            compiler_params=pltpu.CompilerParams(
                collective_id=0, has_side_effects=True, vmem_limit_bytes=32 * 1024 * 1024
            ),
        )(water_depth, velocity, bathymetry, wet_tiles, migration)

    return jax.shard_map(
        step,
        mesh=mesh,
        in_specs=(P("gx", "gy"), P(None, "gx", "gy"), P("gx", "gy"), P("gx", "gy"), P("gx", "gy")),
        out_specs=P(None, "gx", "gy"),
        check_vma=False,
    )
```

```python
import functools

import jax
import jax.numpy as jnp
from jax import lax
from jax.experimental import pallas as pl
from jax.experimental.pallas import tpu as pltpu
from jax.sharding import PartitionSpec as P

DRY_DEPTH = 0.05
COURANT = 0.15
HALO = 4
ROWS = 8
LANES = 128
REACH = 8
WET_LANE = 32
MESH = pl.DeviceIdType.MESH
CORNERS = ((0, 0), (1, 0), (0, 1), (1, 1))


def lanes_of(shape):
    return lax.broadcasted_iota(jnp.int32, shape, len(shape) - 1)


def turn(x, by, axis):
    return pltpu.roll(x, by % x.shape[axis], axis)


def ring_next(tiles):
    turned = [turn(x, -1, 1) for x in tiles]
    last = lanes_of(turned[0].shape) == LANES - 1
    return [jnp.where(last, turned[(c + 1) % len(tiles)], turned[c]) for c in range(len(tiles))]


def ring_previous(tiles):
    turned = [turn(x, 1, 1) for x in tiles]
    first = lanes_of(turned[0].shape) == 0
    return [jnp.where(first, turned[c - 1], turned[c]) for c in range(len(tiles))]


def rates(state):
    parts = []
    for h, p, q in state:
        floored = jnp.maximum(h, DRY_DEPTH)
        inverse_root = lax.rsqrt(floored)
        celerity = floored * inverse_root
        inverse = inverse_root * inverse_root
        u = p * inverse
        v = q * inverse
        pressure = 0.5 * h * h
        parts.append(
            (h, p, q, p * u + pressure, q * u, q * v + pressure, jnp.abs(u) + celerity, jnp.abs(v) + celerity)
        )
    fields = list(zip(*parts))
    h, p, q, east, cross, north, reach_x, reach_y = fields
    on = [ring_next(x) for x in (h, p, q, east, cross, reach_x)]
    faces = [[], [], []]
    for c in range(len(state)):
        wave = jnp.maximum(reach_x[c], on[5][c])
        faces[0].append(p[c] + on[1][c] - wave * (on[0][c] - h[c]))
        faces[1].append(east[c] + on[3][c] - wave * (on[1][c] - p[c]))
        faces[2].append(cross[c] + on[4][c] - wave * (on[2][c] - q[c]))
    back = [ring_previous(x) for x in faces]
    out = []
    for c in range(len(state)):
        below = [turn(x[c], -1, 0) for x in (h, p, q, cross, north, reach_y)]
        wave = jnp.maximum(reach_y[c], below[5])
        rows = (
            q[c] + below[2] - wave * (below[0] - h[c]),
            cross[c] + below[3] - wave * (below[1] - p[c]),
            north[c] + below[4] - wave * (below[2] - q[c]),
        )
        out.append(
            tuple((faces[f][c] - back[f][c]) + (rows[f] - turn(rows[f], 1, 0)) for f in range(3))
        )
    return out


def half_step(state, slopes, masks, start):
    out = []
    changes = rates(state)
    for c, (cells, change, slope, mask) in enumerate(zip(state, changes, slopes, masks)):
        moved = [cells[0] - (0.5 * COURANT) * change[0]]
        for f in (1, 2):
            moved.append(cells[f] - (0.5 * COURANT) * change[f] - cells[0] * slope[f - 1])
        if start is not None:
            moved = [0.5 * start[c][f] + 0.5 * moved[f] for f in range(3)]
        out.append(tuple(x * mask for x in moved))
    return out


def two_steps(state, slopes, masks):
    for _ in range(2):
        middle = half_step(state, slopes, masks, None)
        state = half_step(middle, slopes, masks, state)
    return state


def kernel(
    sizes,
    depth_hbm,
    velocity_hbm,
    bed_hbm,
    wet_hbm,
    migration_hbm,
    out_ref,
    own,
    above,
    below,
    strip,
    strips,
    corners,
    wet,
    homes,
    tiles,
    outgoing,
    arrived,
    load_sem,
    halo_send,
    halo_recv,
    strip_send,
    strip_recv,
    corner_send,
    corner_recv,
    home_send,
    home_recv,
    slot_send,
    slot_recv,
):
    n_rows, n_cols = sizes
    tile_count = own.shape[2] // LANES
    gx, gy = lax.axis_index("gx"), lax.axis_index("gy")
    has_up, has_down, has_left, has_right = gx > 0, gx < n_rows - 1, gy > 0, gy < n_cols - 1
    up, down = lax.rem(gx + n_rows - 1, n_rows), lax.rem(gx + 1, n_rows)
    left, right = lax.rem(gy + n_cols - 1, n_cols), lax.rem(gy + 1, n_cols)
    corner_ids = [((up, down)[r], (left, right)[s]) for r, s in CORNERS]
    has_corner = [(has_up, has_down)[r] & (has_left, has_right)[s] for r, s in CORNERS]

    def row_mate(k):
        return (gx, lax.rem(gy + k, n_cols))

    def remote(source, target, send, receive, where):
        return pltpu.make_async_remote_copy(
            src_ref=source, dst_ref=target, send_sem=send, recv_sem=receive, device_id=where, device_id_type=MESH
        )

    barrier = pltpu.get_barrier_semaphore()

    def greet(friend):
        pl.semaphore_signal(barrier, inc=1, device_id=friend, device_id_type=MESH)

    beyond = [(has_up, (up, gy)), (has_down, (down, gy))] + list(zip(has_corner, corner_ids))
    for there, friend in beyond:
        pl.when(there)(functools.partial(greet, friend))
    for k in range(1, n_cols):
        greet(row_mate(k))
    friends = n_cols - 1 + sum(there.astype(jnp.int32) for there, _ in beyond)

    loads = [
        pltpu.make_async_copy(depth_hbm, own.at[0], load_sem.at[0]),
        pltpu.make_async_copy(velocity_hbm, own.at[pl.ds(1, 2)], load_sem.at[1]),
        pltpu.make_async_copy(bed_hbm, own.at[3], load_sem.at[2]),
        pltpu.make_async_copy(wet_hbm, wet, load_sem.at[3]),
        pltpu.make_async_copy(migration_hbm, homes.at[0], load_sem.at[4]),
    ]
    for load in loads:
        load.start()
    for load in loads:
        load.wait()

    lane = lanes_of((ROWS, LANES))
    packed = jnp.zeros((ROWS, LANES), jnp.float32)
    for f in range(4):
        first, last = own[f, :, 0:LANES], own[f, :, (tile_count - 1) * LANES : tile_count * LANES]
        at = REACH * f
        packed = jnp.where((lane >= at) & (lane < at + REACH), turn(first, at, 1) if f else first, packed)
        at = LANES - REACH * (f + 1)
        packed = jnp.where((lane >= at) & (lane < at + REACH), turn(last, -REACH * f, 1) if f else last, packed)
    for t in range(tile_count):
        packed = jnp.where(lane == WET_LANE + t, wet[0, t].astype(jnp.float32), packed)
    strip[...] = packed

    pl.semaphore_wait(barrier, friends)

    ways = [(has_up, (up, gy), below), (has_down, (down, gy), above), (has_left, (gx, left), None), (has_right, (gx, right), None)]
    halos = []
    for i, (there, where, target) in enumerate(ways):
        copies = [remote(strip, strips.at[i], strip_send.at[i], strip_recv.at[i], where)]
        if target is not None:
            copies.append(remote(own, target, halo_send.at[i], halo_recv.at[i], where))
        halos.append((there, copies))
    for i, (there, where) in enumerate(zip(has_corner, corner_ids)):
        halos.append((there, [remote(strip, corners.at[i], corner_send.at[i], corner_recv.at[i], where)]))
    opposite = [1, 0, 3, 2, 7, 6, 5, 4]
    mates = [
        remote(homes.at[0], homes.at[k], home_send.at[k], home_recv.at[k], row_mate(k)) for k in range(1, n_cols)
    ]

    def each(copies, what):
        for copy in copies:
            getattr(copy, what)()

    for there, copies in halos:
        pl.when(there)(functools.partial(each, copies, "start"))
    each(mates, "start")

    chosen = []
    for k in range(n_cols):
        target = row_mate(k)[1]
        index = jnp.int32(0)
        for t in range(1, tile_count):
            index = jnp.where(homes[0, 0, t] == target, t, index)
        chosen.append(index)

    for (there, _), i in zip(halos, opposite):
        pl.when(there)(functools.partial(each, halos[i][1], "wait_recv"))

    def columns(reference, f):
        return [reference[f, :, c * LANES : (c + 1) * LANES] for c in range(tile_count)]

    def ends(from_left, from_right, f):
        head = turn(from_right, -REACH * f, 1) if f else from_right
        tail = turn(from_left, REACH * f, 1) if f else from_left
        return jnp.where(lane < REACH, head, jnp.where(lane >= LANES - REACH, tail, 0.0))

    lower_right, upper_right, lower_left, upper_left = (corners[i] for i in range(4))
    bands = (
        (above, upper_left, upper_right, strips[1]),
        (own, strips[3], strips[2], strip[...]),
        (below, lower_left, lower_right, strips[0]),
    )
    fields = []
    for f in range(4):
        stacked = [columns(band[0], f) + [ends(band[1], band[2], f)] for band in bands]
        fields.append([jnp.concatenate([s[c] for s in stacked], axis=0) for c in range(tile_count + 1)])

    def spread(tile, at):
        return jnp.broadcast_to(tile[:, at : at + 1], (ROWS, LANES))

    wets = []
    for c in range(tile_count + 1):
        stacked = []
        for _, from_left, from_right, flags in bands:
            if c < tile_count:
                stacked.append(spread(flags, WET_LANE + c))
            else:
                stacked.append(
                    jnp.where(
                        lane < LANES // 2, spread(from_right, WET_LANE), spread(from_left, WET_LANE + tile_count - 1)
                    )
                )
        wets.append(jnp.concatenate(stacked, axis=0))

    row = lax.broadcasted_iota(jnp.int32, (3 * ROWS, LANES), 0)
    wide = lanes_of((3 * ROWS, LANES))
    weights = [there.astype(jnp.float32) for there in (has_up, has_down, has_left, has_right)]
    inside_rows = jnp.where(row < ROWS, weights[0], jnp.where(row >= 2 * ROWS, weights[1], jnp.float32(1)))
    inside_ends = inside_rows * jnp.where(wide < LANES // 2, weights[3], weights[2])
    masks = [inside_rows] * tile_count + [inside_ends]

    depth, across, along, beds = ([jnp.where(m > 0.5, x, 0.0) for m, x in zip(masks, field)] for field in fields)
    state = [(depth[c], depth[c] * across[c], depth[c] * along[c]) for c in range(tile_count + 1)]
    bed_next, bed_previous = ring_next(beds), ring_previous(beds)
    slopes = [
        (
            (0.5 * COURANT) * (bed_next[c] - bed_previous[c]),
            (0.5 * COURANT) * (turn(beds[c], -1, 0) - turn(beds[c], 1, 0)),
        )
        for c in range(tile_count + 1)
    ]
    advanced = two_steps(state, slopes, masks)
    state = [
        tuple(jnp.where(w > 0.5, new, old) for new, old in zip(a, s)) for w, a, s in zip(wets, advanced, state)
    ]

    def narrow(x, start, size):
        return turn(x, -start, 0)[:size]

    kept = 2 * HALO + ROWS
    state = [tuple(narrow(x, ROWS - HALO, kept) for x in s) for s in state]
    slopes = [tuple(narrow(x, ROWS - HALO, kept) for x in s) for s in slopes]
    masks = [narrow(x, ROWS - HALO, kept) for x in masks]
    advanced = two_steps(state, slopes, masks)
    for t in range(tile_count):
        for f in range(3):
            new, old = narrow(advanced[t][f], HALO, ROWS), narrow(state[t][f], HALO, ROWS)
            tiles[t, f] = jnp.where(wets[t][ROWS : 2 * ROWS] > 0.5, new, old)

    slots = []
    for k in sorted(range(1, n_cols), key=lambda k: -min(k, n_cols - k)):
        outgoing[k] = tiles[chosen[k]]
        copy = remote(outgoing.at[k], arrived.at[k], slot_send.at[k], slot_recv.at[k], row_mate(k))
        copy.start()
        slots.append(copy)
    arrived[0] = tiles[chosen[0]]

    each(mates, "wait_recv")
    sources = []
    for t in range(tile_count):
        index = jnp.int32(0)
        for k in range(1, n_cols):
            index = jnp.where(homes[k, 0, t] == gy, k, index)
        sources.append(index)
    each(slots, "wait_recv")
    for t in range(tile_count):
        out_ref[:, :, t * LANES : (t + 1) * LANES] = arrived[sources[t]]
    for there, copies in halos:
        pl.when(there)(functools.partial(each, copies, "wait_send"))
    each(mates + slots, "wait_send")


def solution(mesh):
    n_rows, n_cols = mesh.shape["gx"], mesh.shape["gy"]

    def step(water_depth, velocity, bathymetry, wet_tiles, migration):
        rows, cols = water_depth.shape
        tile_count = wet_tiles.shape[1]
        block = (4, rows, cols)
        dma = pltpu.SemaphoreType.DMA
        return pl.pallas_call(
            functools.partial(kernel, (n_rows, n_cols)),
            out_shape=jax.ShapeDtypeStruct((3, rows, cols), jnp.float32),
            in_specs=[pl.BlockSpec(memory_space=pl.ANY)] * 5,
            out_specs=pl.BlockSpec(memory_space=pltpu.VMEM),
            scratch_shapes=[
                pltpu.VMEM(block, jnp.float32),
                pltpu.VMEM(block, jnp.float32),
                pltpu.VMEM(block, jnp.float32),
                pltpu.VMEM((ROWS, LANES), jnp.float32),
                pltpu.VMEM((4, ROWS, LANES), jnp.float32),
                pltpu.VMEM((4, ROWS, LANES), jnp.float32),
                pltpu.SMEM((1, tile_count), jnp.int32),
                pltpu.SMEM((n_cols, 1, tile_count), jnp.int32),
                pltpu.VMEM((tile_count, 3, rows, LANES), jnp.float32),
                pltpu.VMEM((n_cols, 3, rows, LANES), jnp.float32),
                pltpu.VMEM((n_cols, 3, rows, LANES), jnp.float32),
                dma((5,)),
                dma((2,)),
                dma((2,)),
                dma((4,)),
                dma((4,)),
                dma((4,)),
                dma((4,)),
                dma((n_cols,)),
                dma((n_cols,)),
                dma((n_cols,)),
                dma((n_cols,)),
            ],
            compiler_params=pltpu.CompilerParams(
                collective_id=0, has_side_effects=True, vmem_limit_bytes=60 * 1024 * 1024
            ),
        )(water_depth, velocity, bathymetry, wet_tiles, migration)

    return jax.shard_map(
        step,
        mesh=mesh,
        in_specs=(P("gx", "gy"), P(None, "gx", "gy"), P("gx", "gy"), P("gx", "gy"), P("gx", "gy")),
        out_specs=P(None, "gx", "gy"),
        check_vma=False,
    )
```

```python
import functools

import jax
import jax.numpy as jnp
from jax import lax
from jax.experimental import pallas as pl
from jax.experimental.pallas import tpu as pltpu
from jax.sharding import PartitionSpec as P

DRY_DEPTH = 0.05
COURANT = 0.15
HALO = 4
ROWS = 8
LANES = 128
REACH = 8
WET_LANE = 32
MESH = pl.DeviceIdType.MESH
CORNERS = ((0, 0), (1, 0), (0, 1), (1, 1))


def lanes_of(shape):
    return lax.broadcasted_iota(jnp.int32, shape, len(shape) - 1)


def turn(x, by, axis):
    return pltpu.roll(x, by % x.shape[axis], axis)


def ring_next(tiles):
    turned = [turn(x, -1, 1) for x in tiles]
    last = lanes_of(turned[0].shape) == LANES - 1
    return [jnp.where(last, turned[(c + 1) % len(tiles)], turned[c]) for c in range(len(tiles))]


def ring_previous(tiles):
    turned = [turn(x, 1, 1) for x in tiles]
    first = lanes_of(turned[0].shape) == 0
    return [jnp.where(first, turned[c - 1], turned[c]) for c in range(len(tiles))]


def rates(state):
    parts = []
    for h, p, q in state:
        floored = jnp.maximum(h, DRY_DEPTH)
        inverse_root = lax.rsqrt(floored)
        celerity = floored * inverse_root
        inverse = inverse_root * inverse_root
        u = p * inverse
        v = q * inverse
        pressure = 0.5 * h * h
        parts.append(
            (h, p, q, p * u + pressure, q * u, q * v + pressure, jnp.abs(u) + celerity, jnp.abs(v) + celerity)
        )
    fields = list(zip(*parts))
    h, p, q, east, cross, north, reach_x, reach_y = fields
    on = [ring_next(x) for x in (h, p, q, east, cross, reach_x)]
    faces = [[], [], []]
    for c in range(len(state)):
        wave = jnp.maximum(reach_x[c], on[5][c])
        faces[0].append(p[c] + on[1][c] - wave * (on[0][c] - h[c]))
        faces[1].append(east[c] + on[3][c] - wave * (on[1][c] - p[c]))
        faces[2].append(cross[c] + on[4][c] - wave * (on[2][c] - q[c]))
    back = [ring_previous(x) for x in faces]
    out = []
    for c in range(len(state)):
        below = [turn(x[c], -1, 0) for x in (h, p, q, cross, north, reach_y)]
        wave = jnp.maximum(reach_y[c], below[5])
        rows = (
            q[c] + below[2] - wave * (below[0] - h[c]),
            cross[c] + below[3] - wave * (below[1] - p[c]),
            north[c] + below[4] - wave * (below[2] - q[c]),
        )
        out.append(
            tuple((faces[f][c] - back[f][c]) + (rows[f] - turn(rows[f], 1, 0)) for f in range(3))
        )
    return out


def half_step(state, slopes, masks, start):
    out = []
    changes = rates(state)
    for c, (cells, change, slope, mask) in enumerate(zip(state, changes, slopes, masks)):
        moved = [cells[0] - (0.5 * COURANT) * change[0]]
        for f in (1, 2):
            moved.append(cells[f] - (0.5 * COURANT) * change[f] - cells[0] * slope[f - 1])
        if start is not None:
            moved = [0.5 * start[c][f] + 0.5 * moved[f] for f in range(3)]
        out.append(tuple(x * mask for x in moved))
    return out


def two_steps(state, slopes, masks):
    for _ in range(2):
        middle = half_step(state, slopes, masks, None)
        state = half_step(middle, slopes, masks, state)
    return state


def kernel(
    sizes,
    depth_hbm,
    velocity_hbm,
    bed_hbm,
    wet_hbm,
    migration_hbm,
    out_ref,
    own,
    above,
    below,
    strip,
    strips,
    corners,
    wet,
    homes,
    tiles,
    outgoing,
    arrived,
    load_sem,
    halo_send,
    halo_recv,
    strip_send,
    strip_recv,
    corner_send,
    corner_recv,
    home_send,
    home_recv,
    slot_send,
    slot_recv,
    lower,
    higher,
):
    n_rows, n_cols = sizes
    tile_count = own.shape[2] // LANES
    gx, gy = lax.axis_index("gx"), lax.axis_index("gy")
    has_up, has_down, has_left, has_right = gx > 0, gx < n_rows - 1, gy > 0, gy < n_cols - 1
    up, down = lax.rem(gx + n_rows - 1, n_rows), lax.rem(gx + 1, n_rows)
    left, right = lax.rem(gy + n_cols - 1, n_cols), lax.rem(gy + 1, n_cols)
    corner_ids = [((up, down)[r], (left, right)[s]) for r, s in CORNERS]
    has_corner = [(has_up, has_down)[r] & (has_left, has_right)[s] for r, s in CORNERS]

    def remote(source, target, send, receive, where):
        return pltpu.make_async_remote_copy(
            src_ref=source, dst_ref=target, send_sem=send, recv_sem=receive, device_id=where, device_id_type=MESH
        )

    barrier = pltpu.get_barrier_semaphore()

    def greet(friend):
        pl.semaphore_signal(barrier, inc=1, device_id=friend, device_id_type=MESH)

    beyond = [(has_up, (up, gy)), (has_down, (down, gy)), (has_left, (gx, left)), (has_right, (gx, right))]
    beyond += list(zip(has_corner, corner_ids))
    for there, friend in beyond:
        pl.when(there)(functools.partial(greet, friend))
    friends = sum(there.astype(jnp.int32) for there, _ in beyond)

    loads = [
        pltpu.make_async_copy(depth_hbm, own.at[0], load_sem.at[0]),
        pltpu.make_async_copy(velocity_hbm, own.at[pl.ds(1, 2)], load_sem.at[1]),
        pltpu.make_async_copy(bed_hbm, own.at[3], load_sem.at[2]),
        pltpu.make_async_copy(wet_hbm, wet, load_sem.at[3]),
        pltpu.make_async_copy(migration_hbm, homes.at[gy], load_sem.at[4]),
    ]
    for load in loads:
        load.start()
    for load in loads:
        load.wait()

    lane = lanes_of((ROWS, LANES))
    packed = jnp.zeros((ROWS, LANES), jnp.float32)
    for f in range(4):
        first, last = own[f, :, 0:LANES], own[f, :, (tile_count - 1) * LANES : tile_count * LANES]
        at = REACH * f
        packed = jnp.where((lane >= at) & (lane < at + REACH), turn(first, at, 1) if f else first, packed)
        at = LANES - REACH * (f + 1)
        packed = jnp.where((lane >= at) & (lane < at + REACH), turn(last, -REACH * f, 1) if f else last, packed)
    for t in range(tile_count):
        packed = jnp.where(lane == WET_LANE + t, wet[0, t].astype(jnp.float32), packed)
    strip[...] = packed

    pl.semaphore_wait(barrier, friends)

    ways = [(has_up, (up, gy), below), (has_down, (down, gy), above), (has_left, (gx, left), None), (has_right, (gx, right), None)]
    halos = []
    for i, (there, where, target) in enumerate(ways):
        copies = [remote(strip, strips.at[i], strip_send.at[i], strip_recv.at[i], where)]
        if target is not None:
            copies.append(remote(own, target, halo_send.at[i], halo_recv.at[i], where))
        halos.append((there, copies))
    for i, (there, where) in enumerate(zip(has_corner, corner_ids)):
        halos.append((there, [remote(strip, corners.at[i], corner_send.at[i], corner_recv.at[i], where)]))
    opposite = [1, 0, 3, 2, 7, 6, 5, 4]
    def each(copies, what):
        for copy in copies:
            getattr(copy, what)()

    for there, copies in halos:
        pl.when(there)(functools.partial(each, copies, "start"))

    def send_home(target):
        remote(homes.at[gy], homes.at[gy], home_send, home_recv, (gx, target)).start()

    def announce(target, carry):
        pl.semaphore_signal(higher, inc=1, device_id=(gx, target), device_id_type=MESH)
        send_home(target)
        return carry

    @pl.when(has_left)
    def _():
        pl.semaphore_wait(lower, 1)

    @pl.when(has_right)
    def _():
        pl.semaphore_signal(lower, inc=1, device_id=(gx, right), device_id_type=MESH)

    lax.fori_loop(0, gy, announce, 0)

    chosen = []
    for target in range(n_cols):
        index = jnp.int32(0)
        for t in range(1, tile_count):
            index = jnp.where(homes[gy, 0, t] == target, t, index)
        chosen.append(index)

    for (there, _), i in zip(halos, opposite):
        pl.when(there)(functools.partial(each, halos[i][1], "wait_recv"))

    def columns(reference, f):
        return [reference[f, :, c * LANES : (c + 1) * LANES] for c in range(tile_count)]

    def ends(from_left, from_right, f):
        head = turn(from_right, -REACH * f, 1) if f else from_right
        tail = turn(from_left, REACH * f, 1) if f else from_left
        return jnp.where(lane < REACH, head, jnp.where(lane >= LANES - REACH, tail, 0.0))

    lower_right, upper_right, lower_left, upper_left = (corners[i] for i in range(4))
    bands = (
        (above, upper_left, upper_right, strips[1]),
        (own, strips[3], strips[2], strip[...]),
        (below, lower_left, lower_right, strips[0]),
    )
    fields = []
    for f in range(4):
        stacked = [columns(band[0], f) + [ends(band[1], band[2], f)] for band in bands]
        fields.append([jnp.concatenate([s[c] for s in stacked], axis=0) for c in range(tile_count + 1)])

    def spread(tile, at):
        return jnp.broadcast_to(tile[:, at : at + 1], (ROWS, LANES))

    wets = []
    for c in range(tile_count + 1):
        stacked = []
        for _, from_left, from_right, flags in bands:
            if c < tile_count:
                stacked.append(spread(flags, WET_LANE + c))
            else:
                stacked.append(
                    jnp.where(
                        lane < LANES // 2, spread(from_right, WET_LANE), spread(from_left, WET_LANE + tile_count - 1)
                    )
                )
        wets.append(jnp.concatenate(stacked, axis=0))

    row = lax.broadcasted_iota(jnp.int32, (3 * ROWS, LANES), 0)
    wide = lanes_of((3 * ROWS, LANES))
    weights = [there.astype(jnp.float32) for there in (has_up, has_down, has_left, has_right)]
    inside_rows = jnp.where(row < ROWS, weights[0], jnp.where(row >= 2 * ROWS, weights[1], jnp.float32(1)))
    inside_ends = inside_rows * jnp.where(wide < LANES // 2, weights[3], weights[2])
    masks = [inside_rows] * tile_count + [inside_ends]

    depth, across, along, beds = ([jnp.where(m > 0.5, x, 0.0) for m, x in zip(masks, field)] for field in fields)
    state = [(depth[c], depth[c] * across[c], depth[c] * along[c]) for c in range(tile_count + 1)]
    bed_next, bed_previous = ring_next(beds), ring_previous(beds)
    slopes = [
        (
            (0.5 * COURANT) * (bed_next[c] - bed_previous[c]),
            (0.5 * COURANT) * (turn(beds[c], -1, 0) - turn(beds[c], 1, 0)),
        )
        for c in range(tile_count + 1)
    ]
    advanced = two_steps(state, slopes, masks)
    state = [
        tuple(jnp.where(w > 0.5, new, old) for new, old in zip(a, s)) for w, a, s in zip(wets, advanced, state)
    ]

    def narrow(x, start, size):
        return turn(x, -start, 0)[:size]

    kept = 2 * HALO + ROWS
    state = [tuple(narrow(x, ROWS - HALO, kept) for x in s) for s in state]
    slopes = [tuple(narrow(x, ROWS - HALO, kept) for x in s) for s in slopes]
    masks = [narrow(x, ROWS - HALO, kept) for x in masks]
    advanced = two_steps(state, slopes, masks)
    for t in range(tile_count):
        for f in range(3):
            new, old = narrow(advanced[t][f], HALO, ROWS), narrow(state[t][f], HALO, ROWS)
            tiles[t, f] = jnp.where(wets[t][ROWS : 2 * ROWS] > 0.5, new, old)

    for target in range(n_cols):
        outgoing[target] = tiles[chosen[target]]
    arrived[gy] = outgoing[gy]

    def send_slot(target):
        remote(outgoing.at[target], arrived.at[gy], slot_send, slot_recv, (gx, target)).start()

    def to_lower(target, carry):
        send_slot(target)
        return carry

    def to_higher(target, carry):
        send_home(target)
        send_slot(target)
        return carry

    lax.fori_loop(0, gy, to_lower, 0)

    @pl.when(has_right)
    def _():
        pl.semaphore_wait(higher, n_cols - 1 - gy)

    lax.fori_loop(gy + 1, n_cols, to_higher, 0)

    others = pl.ds(0, n_cols - 1)
    all_homes = remote(homes.at[others], homes.at[others], home_send, home_recv, (gx, right))
    all_slots = remote(outgoing.at[others], arrived.at[others], slot_send, slot_recv, (gx, right))
    all_homes.wait_recv()
    sources = []
    for t in range(tile_count):
        index = jnp.int32(0)
        for source in range(1, n_cols):
            index = jnp.where(homes[source, 0, t] == gy, source, index)
        sources.append(index)
    all_slots.wait_recv()
    for t in range(tile_count):
        out_ref[:, :, t * LANES : (t + 1) * LANES] = arrived[sources[t]]
    for there, copies in halos:
        pl.when(there)(functools.partial(each, copies, "wait_send"))
    all_homes.wait_send()
    all_slots.wait_send()


def solution(mesh):
    n_rows, n_cols = mesh.shape["gx"], mesh.shape["gy"]

    def step(water_depth, velocity, bathymetry, wet_tiles, migration):
        rows, cols = water_depth.shape
        tile_count = wet_tiles.shape[1]
        block = (4, rows, cols)
        dma = pltpu.SemaphoreType.DMA
        return pl.pallas_call(
            functools.partial(kernel, (n_rows, n_cols)),
            out_shape=pltpu.VMEM((3, rows, cols), jnp.float32),
            in_specs=[pl.BlockSpec(memory_space=pl.ANY)] * 5,
            out_specs=pl.BlockSpec(memory_space=pltpu.VMEM),
            scratch_shapes=[
                pltpu.VMEM(block, jnp.float32),
                pltpu.VMEM(block, jnp.float32),
                pltpu.VMEM(block, jnp.float32),
                pltpu.VMEM((ROWS, LANES), jnp.float32),
                pltpu.VMEM((4, ROWS, LANES), jnp.float32),
                pltpu.VMEM((4, ROWS, LANES), jnp.float32),
                pltpu.SMEM((1, tile_count), jnp.int32),
                pltpu.SMEM((n_cols, 1, tile_count), jnp.int32),
                pltpu.VMEM((tile_count, 3, rows, LANES), jnp.float32),
                pltpu.VMEM((n_cols, 3, rows, LANES), jnp.float32),
                pltpu.VMEM((n_cols, 3, rows, LANES), jnp.float32),
                dma((5,)),
                dma((2,)),
                dma((2,)),
                dma((4,)),
                dma((4,)),
                dma((4,)),
                dma((4,)),
                dma,
                dma,
                dma,
                dma,
                pltpu.SemaphoreType.REGULAR,
                pltpu.SemaphoreType.REGULAR,
            ],
            compiler_params=pltpu.CompilerParams(
                collective_id=0, has_side_effects=True, vmem_limit_bytes=32 * 1024 * 1024
            ),
        )(*(pltpu.with_memory_space_constraint(x, pltpu.HBM) for x in (water_depth, velocity, bathymetry, wet_tiles, migration)))

    return jax.shard_map(
        step,
        mesh=mesh,
        in_specs=(P("gx", "gy"), P(None, "gx", "gy"), P("gx", "gy"), P("gx", "gy"), P("gx", "gy")),
        out_specs=P(None, "gx", "gy"),
        check_vma=False,
    )
```

```python
import functools

import jax
import jax.numpy as jnp
from jax import lax
from jax.experimental import pallas as pl
from jax.experimental.pallas import tpu as pltpu
from jax.sharding import PartitionSpec as P

DRY_DEPTH = 0.05
COURANT = 0.15
HALO = 4
ROWS = 8
LANES = 128
TAG = 3 * ROWS
REACH = 8
WET_LANE = 32
MESH = pl.DeviceIdType.MESH
CORNERS = ((0, 0), (1, 0), (0, 1), (1, 1))


def lanes_of(shape):
    return lax.broadcasted_iota(jnp.int32, shape, len(shape) - 1)


def turn(x, by, axis):
    return pltpu.roll(x, by % x.shape[axis], axis)


def ring_next(tiles):
    turned = [turn(x, -1, 1) for x in tiles]
    last = lanes_of(turned[0].shape) == LANES - 1
    return [jnp.where(last, turned[(c + 1) % len(tiles)], turned[c]) for c in range(len(tiles))]


def ring_previous(tiles):
    turned = [turn(x, 1, 1) for x in tiles]
    first = lanes_of(turned[0].shape) == 0
    return [jnp.where(first, turned[c - 1], turned[c]) for c in range(len(tiles))]


def rates(state):
    parts = []
    for h, p, q in state:
        floored = jnp.maximum(h, DRY_DEPTH)
        inverse_root = lax.rsqrt(floored)
        celerity = floored * inverse_root
        inverse = inverse_root * inverse_root
        u = p * inverse
        v = q * inverse
        pressure = 0.5 * h * h
        parts.append(
            (h, p, q, p * u + pressure, q * u, q * v + pressure, jnp.abs(u) + celerity, jnp.abs(v) + celerity)
        )
    fields = list(zip(*parts))
    h, p, q, east, cross, north, reach_x, reach_y = fields
    on = [ring_next(x) for x in (h, p, q, east, cross, reach_x)]
    faces = [[], [], []]
    for c in range(len(state)):
        wave = jnp.maximum(reach_x[c], on[5][c])
        faces[0].append(p[c] + on[1][c] - wave * (on[0][c] - h[c]))
        faces[1].append(east[c] + on[3][c] - wave * (on[1][c] - p[c]))
        faces[2].append(cross[c] + on[4][c] - wave * (on[2][c] - q[c]))
    back = [ring_previous(x) for x in faces]
    out = []
    for c in range(len(state)):
        below = [turn(x[c], -1, 0) for x in (h, p, q, cross, north, reach_y)]
        wave = jnp.maximum(reach_y[c], below[5])
        rows = (
            q[c] + below[2] - wave * (below[0] - h[c]),
            cross[c] + below[3] - wave * (below[1] - p[c]),
            north[c] + below[4] - wave * (below[2] - q[c]),
        )
        out.append(
            tuple((faces[f][c] - back[f][c]) + (rows[f] - turn(rows[f], 1, 0)) for f in range(3))
        )
    return out


def half_step(state, slopes, masks, start):
    out = []
    changes = rates(state)
    for c, (cells, change, slope, mask) in enumerate(zip(state, changes, slopes, masks)):
        moved = [cells[0] - (0.5 * COURANT) * change[0]]
        for f in (1, 2):
            moved.append(cells[f] - (0.5 * COURANT) * change[f] - cells[0] * slope[f - 1])
        if start is not None:
            moved = [0.5 * start[c][f] + 0.5 * moved[f] for f in range(3)]
        out.append(tuple(x * mask for x in moved))
    return out


def two_steps(state, slopes, masks):
    for _ in range(2):
        middle = half_step(state, slopes, masks, None)
        state = half_step(middle, slopes, masks, state)
    return state


def kernel(
    sizes,
    depth_hbm,
    velocity_hbm,
    bed_hbm,
    wet_hbm,
    migration_hbm,
    out_ref,
    own,
    above,
    below,
    strip,
    strips,
    corners,
    wet,
    migration,
    tiles,
    outgoing,
    arrived,
    load_sem,
    halo_send,
    halo_recv,
    strip_send,
    strip_recv,
    corner_send,
    corner_recv,
    slot_send,
    slot_recv,
    lower,
    higher,
):
    n_rows, n_cols = sizes
    tile_count = own.shape[2] // LANES
    gx, gy = lax.axis_index("gx"), lax.axis_index("gy")
    has_up, has_down, has_left, has_right = gx > 0, gx < n_rows - 1, gy > 0, gy < n_cols - 1
    up, down = lax.rem(gx + n_rows - 1, n_rows), lax.rem(gx + 1, n_rows)
    left, right = lax.rem(gy + n_cols - 1, n_cols), lax.rem(gy + 1, n_cols)
    corner_ids = [((up, down)[r], (left, right)[s]) for r, s in CORNERS]
    has_corner = [(has_up, has_down)[r] & (has_left, has_right)[s] for r, s in CORNERS]

    def remote(source, target, send, receive, where):
        return pltpu.make_async_remote_copy(
            src_ref=source, dst_ref=target, send_sem=send, recv_sem=receive, device_id=where, device_id_type=MESH
        )

    barrier = pltpu.get_barrier_semaphore()

    def greet(friend):
        pl.semaphore_signal(barrier, inc=1, device_id=friend, device_id_type=MESH)

    beyond = [(has_up, (up, gy)), (has_down, (down, gy)), (has_left, (gx, left)), (has_right, (gx, right))]
    beyond += list(zip(has_corner, corner_ids))
    second = lax.rem(gy, 2) == 1
    beyond += [(second & (gy >= 2), (gx, lax.rem(gy + n_cols - 2, n_cols)))]
    beyond += [(second & (gy + 2 < n_cols), (gx, lax.rem(gy + 2, n_cols)))]
    for there, friend in beyond:
        pl.when(there)(functools.partial(greet, friend))
    friends = sum(there.astype(jnp.int32) for there, _ in beyond)

    loads = [
        pltpu.make_async_copy(depth_hbm, own.at[0], load_sem.at[0]),
        pltpu.make_async_copy(velocity_hbm, own.at[pl.ds(1, 2)], load_sem.at[1]),
        pltpu.make_async_copy(bed_hbm, own.at[3], load_sem.at[2]),
        pltpu.make_async_copy(wet_hbm, wet, load_sem.at[3]),
        pltpu.make_async_copy(migration_hbm, migration, load_sem.at[4]),
    ]
    for load in loads:
        load.start()
    for load in loads:
        load.wait()

    lane = lanes_of((ROWS, LANES))
    packed = jnp.zeros((ROWS, LANES), jnp.float32)
    for f in range(4):
        first, last = own[f, :, 0:LANES], own[f, :, (tile_count - 1) * LANES : tile_count * LANES]
        at = REACH * f
        packed = jnp.where((lane >= at) & (lane < at + REACH), turn(first, at, 1) if f else first, packed)
        at = LANES - REACH * (f + 1)
        packed = jnp.where((lane >= at) & (lane < at + REACH), turn(last, -REACH * f, 1) if f else last, packed)
    for t in range(tile_count):
        packed = jnp.where(lane == WET_LANE + t, wet[0, t].astype(jnp.float32), packed)
    strip[...] = packed

    pl.semaphore_wait(barrier, friends)

    ways = [(has_up, (up, gy), below), (has_down, (down, gy), above), (has_left, (gx, left), None), (has_right, (gx, right), None)]
    halos = []
    for i, (there, where, target) in enumerate(ways):
        copies = [remote(strip, strips.at[i], strip_send.at[i], strip_recv.at[i], where)]
        if target is not None:
            copies.append(remote(own, target, halo_send.at[i], halo_recv.at[i], where))
        halos.append((there, copies))
    for i, (there, where) in enumerate(zip(has_corner, corner_ids)):
        halos.append((there, [remote(strip, corners.at[i], corner_send.at[i], corner_recv.at[i], where)]))
    opposite = [1, 0, 3, 2, 7, 6, 5, 4]
    def each(copies, what):
        for copy in copies:
            getattr(copy, what)()

    for there, copies in halos:
        pl.when(there)(functools.partial(each, copies, "start"))

    @pl.when(gy >= 2)
    def _():
        pl.semaphore_wait(lower, 1)

    def pass_on(target):
        pl.semaphore_signal(lower, inc=1, device_id=(gx, target), device_id_type=MESH)

    pl.when(second & has_right)(functools.partial(pass_on, right))
    pl.when(second & (gy + 2 < n_cols))(functools.partial(pass_on, lax.rem(gy + 2, n_cols)))

    def announce(target, carry):
        pl.semaphore_signal(higher, inc=1, device_id=(gx, target), device_id_type=MESH)
        return carry

    lax.fori_loop(0, gy, announce, 0)

    chosen = []
    for target in range(n_cols):
        index = jnp.int32(-1)
        for t in range(tile_count):
            index = jnp.where(migration[0, t] == target, t, index)
        chosen.append(index)

    for (there, _), i in zip(halos, opposite):
        pl.when(there)(functools.partial(each, halos[i][1], "wait_recv"))

    def columns(reference, f):
        return [reference[f, :, c * LANES : (c + 1) * LANES] for c in range(tile_count)]

    def ends(from_left, from_right, f):
        head = turn(from_right, -REACH * f, 1) if f else from_right
        tail = turn(from_left, REACH * f, 1) if f else from_left
        return jnp.where(lane < REACH, head, jnp.where(lane >= LANES - REACH, tail, 0.0))

    lower_right, upper_right, lower_left, upper_left = (corners[i] for i in range(4))
    bands = (
        (above, upper_left, upper_right, strips[1]),
        (own, strips[3], strips[2], strip[...]),
        (below, lower_left, lower_right, strips[0]),
    )
    fields = []
    for f in range(4):
        stacked = [columns(band[0], f) + [ends(band[1], band[2], f)] for band in bands]
        fields.append([jnp.concatenate([s[c] for s in stacked], axis=0) for c in range(tile_count + 1)])

    def spread(tile, at):
        return jnp.broadcast_to(tile[:, at : at + 1], (ROWS, LANES))

    wets = []
    for c in range(tile_count + 1):
        stacked = []
        for _, from_left, from_right, flags in bands:
            if c < tile_count:
                stacked.append(spread(flags, WET_LANE + c))
            else:
                stacked.append(
                    jnp.where(
                        lane < LANES // 2, spread(from_right, WET_LANE), spread(from_left, WET_LANE + tile_count - 1)
                    )
                )
        wets.append(jnp.concatenate(stacked, axis=0))

    row = lax.broadcasted_iota(jnp.int32, (3 * ROWS, LANES), 0)
    wide = lanes_of((3 * ROWS, LANES))
    weights = [there.astype(jnp.float32) for there in (has_up, has_down, has_left, has_right)]
    inside_rows = jnp.where(row < ROWS, weights[0], jnp.where(row >= 2 * ROWS, weights[1], jnp.float32(1)))
    inside_ends = inside_rows * jnp.where(wide < LANES // 2, weights[3], weights[2])
    masks = [inside_rows] * tile_count + [inside_ends]

    depth, across, along, beds = ([jnp.where(m > 0.5, x, 0.0) for m, x in zip(masks, field)] for field in fields)
    state = [(depth[c], depth[c] * across[c], depth[c] * along[c]) for c in range(tile_count + 1)]
    bed_next, bed_previous = ring_next(beds), ring_previous(beds)
    slopes = [
        (
            (0.5 * COURANT) * (bed_next[c] - bed_previous[c]),
            (0.5 * COURANT) * (turn(beds[c], -1, 0) - turn(beds[c], 1, 0)),
        )
        for c in range(tile_count + 1)
    ]
    advanced = two_steps(state, slopes, masks)
    state = [
        tuple(jnp.where(w > 0.5, new, old) for new, old in zip(a, s)) for w, a, s in zip(wets, advanced, state)
    ]

    def narrow(x, start, size):
        return turn(x, -start, 0)[:size]

    kept = 2 * HALO + ROWS
    state = [tuple(narrow(x, ROWS - HALO, kept) for x in s) for s in state]
    slopes = [tuple(narrow(x, ROWS - HALO, kept) for x in s) for s in slopes]
    masks = [narrow(x, ROWS - HALO, kept) for x in masks]
    advanced = two_steps(state, slopes, masks)
    for t in range(tile_count):
        for f in range(3):
            new, old = narrow(advanced[t][f], HALO, ROWS), narrow(state[t][f], HALO, ROWS)
            tiles[t, f * ROWS : (f + 1) * ROWS] = jnp.where(wets[t][ROWS : 2 * ROWS] > 0.5, new, old)

    for target in range(n_cols):
        outgoing[target, : 3 * ROWS] = tiles[jnp.maximum(chosen[target], 0)]
        outgoing[target, TAG : TAG + 1] = jnp.full((1, LANES), chosen[target].astype(jnp.float32))
    arrived[gy] = outgoing[gy]

    slot = pl.ds(0, TAG + 1)

    def send_slot(target, carry):
        remote(outgoing.at[target, slot], arrived.at[gy, slot], slot_send, slot_recv, (gx, target)).start()
        return carry

    lax.fori_loop(0, gy, send_slot, 0)

    @pl.when(has_right)
    def _():
        pl.semaphore_wait(higher, n_cols - 1 - gy)

    lax.fori_loop(gy + 1, n_cols, send_slot, 0)

    others = pl.ds(0, n_cols - 1)
    all_slots = remote(outgoing.at[others, slot], arrived.at[others, slot], slot_send, slot_recv, (gx, right))
    all_slots.wait_recv()
    placed = [[jnp.zeros((ROWS, LANES), jnp.float32) for _ in range(3)] for _ in range(tile_count)]
    for source in range(n_cols):
        tag = jnp.broadcast_to(arrived[source, TAG : TAG + 1], (ROWS, LANES))
        cells = [arrived[source, f * ROWS : (f + 1) * ROWS] for f in range(3)]
        for t in range(tile_count):
            here = tag == jnp.float32(t)
            placed[t] = [jnp.where(here, new, old) for new, old in zip(cells, placed[t])]
    for t in range(tile_count):
        for f in range(3):
            out_ref[f, :, t * LANES : (t + 1) * LANES] = placed[t][f]
    for there, copies in halos:
        pl.when(there)(functools.partial(each, copies, "wait_send"))
    all_slots.wait_send()


def solution(mesh):
    n_rows, n_cols = mesh.shape["gx"], mesh.shape["gy"]

    def step(water_depth, velocity, bathymetry, wet_tiles, migration):
        rows, cols = water_depth.shape
        tile_count = wet_tiles.shape[1]
        block = (4, rows, cols)
        dma = pltpu.SemaphoreType.DMA
        return pl.pallas_call(
            functools.partial(kernel, (n_rows, n_cols)),
            out_shape=pltpu.VMEM((3, rows, cols), jnp.float32),
            in_specs=[pl.BlockSpec(memory_space=pl.ANY)] * 5,
            out_specs=pl.BlockSpec(memory_space=pltpu.VMEM),
            scratch_shapes=[
                pltpu.VMEM(block, jnp.float32),
                pltpu.VMEM(block, jnp.float32),
                pltpu.VMEM(block, jnp.float32),
                pltpu.VMEM((ROWS, LANES), jnp.float32),
                pltpu.VMEM((4, ROWS, LANES), jnp.float32),
                pltpu.VMEM((4, ROWS, LANES), jnp.float32),
                pltpu.SMEM((1, tile_count), jnp.int32),
                pltpu.SMEM((1, tile_count), jnp.int32),
                pltpu.VMEM((tile_count, 3 * rows, LANES), jnp.float32),
                pltpu.VMEM((n_cols, 4 * rows, LANES), jnp.float32),
                pltpu.VMEM((n_cols, 4 * rows, LANES), jnp.float32),
                dma((5,)),
                dma((2,)),
                dma((2,)),
                dma((4,)),
                dma((4,)),
                dma((4,)),
                dma((4,)),
                dma,
                dma,
                pltpu.SemaphoreType.REGULAR,
                pltpu.SemaphoreType.REGULAR,
            ],
            compiler_params=pltpu.CompilerParams(
                collective_id=0, has_side_effects=True, vmem_limit_bytes=32 * 1024 * 1024
            ),
        )(*(pltpu.with_memory_space_constraint(x, pltpu.HBM) for x in (water_depth, velocity, bathymetry, wet_tiles, migration)))

    return jax.shard_map(
        step,
        mesh=mesh,
        in_specs=(P("gx", "gy"), P(None, "gx", "gy"), P("gx", "gy"), P("gx", "gy"), P("gx", "gy")),
        out_specs=P(None, "gx", "gy"),
        check_vma=False,
    )
```

```python
import functools

import jax
import jax.numpy as jnp
from jax import lax
from jax.experimental import pallas as pl
from jax.experimental.pallas import tpu as pltpu
from jax.sharding import PartitionSpec as P

DRY_DEPTH = 0.05
COURANT = 0.15
HALO = 4
ROWS = 8
LANES = 128
TAG = 3 * ROWS
GROUP, GROUP_2 = 2, 2
REACH = 8
WET_LANE = 32
MESH = pl.DeviceIdType.MESH
CORNERS = ((0, 0), (1, 0), (0, 1), (1, 1))


def lanes_of(shape):
    return lax.broadcasted_iota(jnp.int32, shape, len(shape) - 1)


def turn(x, by, axis):
    return pltpu.roll(x, by % x.shape[axis], axis)


def ring_next(x):
    turned = turn(x, -1, 2)
    after = jnp.concatenate([turned[1:], turned[:1]], axis=0)
    return jnp.where(lanes_of(x.shape) == LANES - 1, after, turned)


def ring_previous(x):
    turned = turn(x, 1, 2)
    before = jnp.concatenate([turned[-1:], turned[:-1]], axis=0)
    return jnp.where(lanes_of(x.shape) == 0, before, turned)


def by_group(function, group, arrays):
    count = arrays[0].shape[0]
    pieces = [function(*(x[at : at + group] for x in arrays)) for at in range(0, count, group)]
    return [jnp.concatenate(column, axis=0) for column in zip(*pieces)]


def fluxes(h, p, q):
    floored = jnp.maximum(h, DRY_DEPTH)
    inverse_root = lax.rsqrt(floored)
    celerity = floored * inverse_root
    inverse = inverse_root * inverse_root
    u = p * inverse
    v = q * inverse
    pressure = 0.5 * h * h
    east, cross, north = p * u + pressure, q * u, q * v + pressure
    speed = jnp.abs(u) + celerity
    turned = tuple(turn(x, -1, 2) for x in (h, p, q, east, cross, speed))
    return (east, cross, speed, north, jnp.abs(v) + celerity) + turned


def faces(h, p, q, flux_h, flux_p, flux_q, speed, h_on, p_on, q_on, flux_h_on, flux_p_on, flux_q_on, speed_on):
    wave = jnp.maximum(speed, speed_on)
    return (
        flux_h + flux_h_on - wave * (h_on - h),
        flux_p + flux_p_on - wave * (p_on - p),
        flux_q + flux_q_on - wave * (q_on - q),
    )


def column_faces(h, p, q, east, cross, speed, *turned):
    count = h.shape[0]
    last = lanes_of(h.shape) == LANES - 1
    h_on, p_on, q_on, east_on, cross_on, speed_on = (
        jnp.where(last, after, x) for x, after in zip(turned[:6], turned[6:])
    )
    values = faces(h, p, q, p, east, cross, speed, h_on, p_on, q_on, p_on, east_on, cross_on, speed_on)
    return values + tuple(turn(x, 1, 2) for x in values)


def update(h, p, q, cross, north, speed, *rest):
    columns, slopes, mask, start = rest[:9], rest[9:11], rest[11], rest[12:]
    hb, pb, qb, cross_b, north_b, speed_b = (turn(x, -1, 1) for x in (h, p, q, cross, north, speed))
    rows = faces(h, p, q, q, cross, north, speed, hb, pb, qb, qb, cross_b, north_b, speed_b)
    first = lanes_of(h.shape) == 0
    moved = []
    for f, cells in enumerate((h, p, q)):
        face, back, before = columns[f::3]
        change = (face - jnp.where(first, before, back)) + (rows[f] - turn(rows[f], 1, 1))
        new = cells - (0.5 * COURANT) * change
        if f:
            new = new - h * slopes[f - 1]
        if start:
            new = 0.5 * start[f] + 0.5 * new
        moved.append(new * mask)
    return moved


def half_step(state, slopes, masks, start):
    h, p, q = state
    group = GROUP if h.shape[1] > 2 * ROWS else GROUP_2
    east, cross, reach_x, north, reach_y, *turned = by_group(fluxes, group, state)
    here = [h, p, q, east, cross, reach_x]
    after = [jnp.concatenate([x[1:], x[:1]], axis=0) for x in turned]
    columns = by_group(column_faces, group, here + turned + after)
    before = [jnp.concatenate([x[-1:], x[:-1]], axis=0) for x in columns[3:]]
    others = columns + before + list(slopes) + [masks] + list(start or ())
    return by_group(update, group, [h, p, q, cross, north, reach_y] + others)


def two_steps(state, slopes, masks):
    for _ in range(2):
        middle = half_step(state, slopes, masks, None)
        state = half_step(middle, slopes, masks, state)
    return state


def kernel(
    sizes,
    depth_hbm,
    velocity_hbm,
    bed_hbm,
    wet_hbm,
    migration_hbm,
    out_ref,
    own,
    above,
    below,
    strip,
    strips,
    corners,
    wet,
    migration,
    tiles,
    outgoing,
    arrived,
    load_sem,
    halo_send,
    halo_recv,
    strip_send,
    strip_recv,
    corner_send,
    corner_recv,
    slot_send,
    slot_recv,
    lower,
    higher,
):
    n_rows, n_cols = sizes
    tile_count = own.shape[2] // LANES
    gx, gy = lax.axis_index("gx"), lax.axis_index("gy")
    has_up, has_down, has_left, has_right = gx > 0, gx < n_rows - 1, gy > 0, gy < n_cols - 1
    up, down = lax.rem(gx + n_rows - 1, n_rows), lax.rem(gx + 1, n_rows)
    left, right = lax.rem(gy + n_cols - 1, n_cols), lax.rem(gy + 1, n_cols)
    corner_ids = [((up, down)[r], (left, right)[s]) for r, s in CORNERS]
    has_corner = [(has_up, has_down)[r] & (has_left, has_right)[s] for r, s in CORNERS]

    def remote(source, target, send, receive, where):
        return pltpu.make_async_remote_copy(
            src_ref=source, dst_ref=target, send_sem=send, recv_sem=receive, device_id=where, device_id_type=MESH
        )

    barrier = pltpu.get_barrier_semaphore()

    def greet(friend):
        pl.semaphore_signal(barrier, inc=1, device_id=friend, device_id_type=MESH)

    beyond = [(has_up, (up, gy)), (has_down, (down, gy)), (has_left, (gx, left)), (has_right, (gx, right))]
    beyond += list(zip(has_corner, corner_ids))

    for there, friend in beyond:
        pl.when(there)(functools.partial(greet, friend))
    friends = sum(there.astype(jnp.int32) for there, _ in beyond)

    loads = [
        pltpu.make_async_copy(depth_hbm, own.at[0], load_sem.at[0]),
        pltpu.make_async_copy(velocity_hbm, own.at[pl.ds(1, 2)], load_sem.at[1]),
        pltpu.make_async_copy(bed_hbm, own.at[3], load_sem.at[2]),
        pltpu.make_async_copy(wet_hbm, wet, load_sem.at[3]),
        pltpu.make_async_copy(migration_hbm, migration, load_sem.at[4]),
    ]
    for load in loads:
        load.start()
    for load in loads[:3]:
        load.wait()

    pl.semaphore_wait(barrier, friends)

    def each(copies, what):
        for copy in copies:
            getattr(copy, what)()

    ways = [(has_up, (up, gy), below), (has_down, (down, gy), above), (has_left, (gx, left), None), (has_right, (gx, right), None)]
    halos = []
    for i, (there, where, target) in enumerate(ways):
        copies = []
        if target is not None:
            copies.append(remote(own, target, halo_send.at[i], halo_recv.at[i], where))
            pl.when(there)(functools.partial(each, copies, "start"))
        halos.append((there, copies))

    for load in loads[3:]:
        load.wait()

    lane = lanes_of((ROWS, LANES))
    packed = jnp.zeros((ROWS, LANES), jnp.float32)
    for f in range(4):
        first, last = own[f, :, 0:LANES], own[f, :, (tile_count - 1) * LANES : tile_count * LANES]
        at = REACH * f
        packed = jnp.where((lane >= at) & (lane < at + REACH), turn(first, at, 1) if f else first, packed)
        at = LANES - REACH * (f + 1)
        packed = jnp.where((lane >= at) & (lane < at + REACH), turn(last, -REACH * f, 1) if f else last, packed)
    for t in range(tile_count):
        packed = jnp.where(lane == WET_LANE + t, wet[0, t].astype(jnp.float32), packed)
    strip[...] = packed

    for i, (there, where, _) in enumerate(ways):
        copy = remote(strip, strips.at[i], strip_send.at[i], strip_recv.at[i], where)
        pl.when(there)(copy.start)
        halos[i][1].append(copy)
    for i, (there, where) in enumerate(zip(has_corner, corner_ids)):
        copy = remote(strip, corners.at[i], corner_send.at[i], corner_recv.at[i], where)
        pl.when(there)(copy.start)
        halos.append((there, [copy]))
    opposite = [1, 0, 3, 2, 7, 6, 5, 4]
    @pl.when(has_left)
    def _():
        pl.semaphore_wait(lower, 1)

    @pl.when(has_right)
    def _():
        pl.semaphore_signal(lower, inc=1, device_id=(gx, right), device_id_type=MESH)

    def announce(target, carry):
        pl.semaphore_signal(higher, inc=1, device_id=(gx, target), device_id_type=MESH)
        return carry

    lax.fori_loop(0, gy, announce, 0)

    chosen = []
    for target in range(n_cols):
        index = jnp.int32(-1)
        for t in range(tile_count):
            index = jnp.where(migration[0, t] == target, t, index)
        chosen.append(index)

    for (there, _), i in zip(halos, opposite):
        pl.when(there)(functools.partial(each, halos[i][1], "wait_recv"))

    def columns(reference, f):
        return [reference[f, :, c * LANES : (c + 1) * LANES] for c in range(tile_count)]

    def ends(from_left, from_right, f):
        head = turn(from_right, -REACH * f, 1) if f else from_right
        tail = turn(from_left, REACH * f, 1) if f else from_left
        return jnp.where(lane < REACH, head, jnp.where(lane >= LANES - REACH, tail, 0.0))

    lower_right, upper_right, lower_left, upper_left = (corners[i] for i in range(4))
    bands = (
        (above, upper_left, upper_right, strips[1]),
        (own, strips[3], strips[2], strip[...]),
        (below, lower_left, lower_right, strips[0]),
    )
    fields = []
    for f in range(4):
        stacked = [columns(band[0], f) + [ends(band[1], band[2], f)] for band in bands]
        fields.append([jnp.concatenate([s[c] for s in stacked], axis=0) for c in range(tile_count + 1)])

    def spread(tile, at):
        return jnp.broadcast_to(tile[:, at : at + 1], (ROWS, LANES))

    wets = []
    for c in range(tile_count + 1):
        stacked = []
        for _, from_left, from_right, flags in bands:
            if c < tile_count:
                stacked.append(spread(flags, WET_LANE + c))
            else:
                stacked.append(
                    jnp.where(
                        lane < LANES // 2, spread(from_right, WET_LANE), spread(from_left, WET_LANE + tile_count - 1)
                    )
                )
        wets.append(jnp.concatenate(stacked, axis=0))

    row = lax.broadcasted_iota(jnp.int32, (3 * ROWS, LANES), 0)
    wide = lanes_of((3 * ROWS, LANES))
    weights = [there.astype(jnp.float32) for there in (has_up, has_down, has_left, has_right)]
    inside_rows = jnp.where(row < ROWS, weights[0], jnp.where(row >= 2 * ROWS, weights[1], jnp.float32(1)))
    inside_ends = inside_rows * jnp.where(wide < LANES // 2, weights[3], weights[2])
    masks = [inside_rows] * tile_count + [inside_ends]

    masks = jnp.stack(masks)
    depth, across, along, beds = (jnp.where(masks > 0.5, jnp.stack(field), 0.0) for field in fields)
    state = (depth, depth * across, depth * along)
    slopes = (
        (0.5 * COURANT) * (ring_next(beds) - ring_previous(beds)),
        (0.5 * COURANT) * (turn(beds, -1, 1) - turn(beds, 1, 1)),
    )
    wets = jnp.stack(wets)
    advanced = two_steps(state, slopes, masks)
    state = tuple(jnp.where(wets > 0.5, new, old) for new, old in zip(advanced, state))

    def narrow(x, start, size):
        return turn(x, -start, 1)[:, :size]

    kept = 2 * HALO + ROWS
    state = tuple(narrow(x, ROWS - HALO, kept) for x in state)
    slopes = tuple(narrow(x, ROWS - HALO, kept) for x in slopes)
    advanced = two_steps(state, slopes, narrow(masks, ROWS - HALO, kept))
    wet = wets[:tile_count, ROWS : 2 * ROWS] > 0.5
    for f in range(3):
        new, old = narrow(advanced[f], HALO, ROWS)[:tile_count], narrow(state[f], HALO, ROWS)[:tile_count]
        tiles[:, f * ROWS : (f + 1) * ROWS] = jnp.where(wet, new, old)

    for target in range(n_cols):
        outgoing[target, : 3 * ROWS] = tiles[jnp.maximum(chosen[target], 0)]
        outgoing[target, TAG : TAG + 1] = jnp.full((1, LANES), chosen[target].astype(jnp.float32))
    arrived[gy] = outgoing[gy]

    slot = pl.ds(0, TAG + 1)

    def send_slot(target, carry):
        remote(outgoing.at[target, slot], arrived.at[gy, slot], slot_send, slot_recv, (gx, target)).start()
        return carry

    lax.fori_loop(0, gy, send_slot, 0)

    @pl.when(has_right)
    def _():
        pl.semaphore_wait(higher, n_cols - 1 - gy)

    lax.fori_loop(gy + 1, n_cols, send_slot, 0)

    others = pl.ds(0, n_cols - 1)
    all_slots = remote(outgoing.at[others, slot], arrived.at[others, slot], slot_send, slot_recv, (gx, right))
    all_slots.wait_recv()
    placed = [[jnp.zeros((ROWS, LANES), jnp.float32) for _ in range(3)] for _ in range(tile_count)]
    for source in range(n_cols):
        tag = jnp.broadcast_to(arrived[source, TAG : TAG + 1], (ROWS, LANES))
        cells = [arrived[source, f * ROWS : (f + 1) * ROWS] for f in range(3)]
        for t in range(tile_count):
            here = tag == jnp.float32(t)
            placed[t] = [jnp.where(here, new, old) for new, old in zip(cells, placed[t])]
    for t in range(tile_count):
        for f in range(3):
            out_ref[f, :, t * LANES : (t + 1) * LANES] = placed[t][f]
    for there, copies in halos:
        pl.when(there)(functools.partial(each, copies, "wait_send"))
    all_slots.wait_send()


def solution(mesh):
    n_rows, n_cols = mesh.shape["gx"], mesh.shape["gy"]

    def step(water_depth, velocity, bathymetry, wet_tiles, migration):
        rows, cols = water_depth.shape
        tile_count = wet_tiles.shape[1]
        block = (4, rows, cols)
        dma = pltpu.SemaphoreType.DMA
        return pl.pallas_call(
            functools.partial(kernel, (n_rows, n_cols)),
            out_shape=pltpu.VMEM((3, rows, cols), jnp.float32),
            in_specs=[pl.BlockSpec(memory_space=pl.ANY)] * 5,
            out_specs=pl.BlockSpec(memory_space=pltpu.VMEM),
            scratch_shapes=[
                pltpu.VMEM(block, jnp.float32),
                pltpu.VMEM(block, jnp.float32),
                pltpu.VMEM(block, jnp.float32),
                pltpu.VMEM((ROWS, LANES), jnp.float32),
                pltpu.VMEM((4, ROWS, LANES), jnp.float32),
                pltpu.VMEM((4, ROWS, LANES), jnp.float32),
                pltpu.SMEM((1, tile_count), jnp.int32),
                pltpu.SMEM((1, tile_count), jnp.int32),
                pltpu.VMEM((tile_count, 3 * rows, LANES), jnp.float32),
                pltpu.VMEM((n_cols, 4 * rows, LANES), jnp.float32),
                pltpu.VMEM((n_cols, 4 * rows, LANES), jnp.float32),
                dma((5,)),
                dma((2,)),
                dma((2,)),
                dma((4,)),
                dma((4,)),
                dma((4,)),
                dma((4,)),
                dma,
                dma,
                pltpu.SemaphoreType.REGULAR,
                pltpu.SemaphoreType.REGULAR,
            ],
            compiler_params=pltpu.CompilerParams(
                collective_id=0, has_side_effects=True, vmem_limit_bytes=32 * 1024 * 1024
            ),
        )(*(pltpu.with_memory_space_constraint(x, pltpu.HBM) for x in (water_depth, velocity, bathymetry, wet_tiles, migration)))

    return jax.shard_map(
        step,
        mesh=mesh,
        in_specs=(P("gx", "gy"), P(None, "gx", "gy"), P("gx", "gy"), P("gx", "gy"), P("gx", "gy")),
        out_specs=P(None, "gx", "gy"),
        check_vma=False,
    )
```

```python
import functools

import jax
import jax.numpy as jnp
from jax import lax
from jax.experimental import pallas as pl
from jax.experimental.pallas import tpu as pltpu
from jax.sharding import PartitionSpec as P

DRY_DEPTH = 0.05
COURANT = 0.15
SCALE = 0.5 * COURANT
HALO = 4
ROWS = 8
LANES = 128
TAG = 3 * ROWS
GROUP, GROUP_2 = 2, 2
REACH = 8
WET_LANE = 32
MESH = pl.DeviceIdType.MESH
CORNERS = ((0, 0), (1, 0), (0, 1), (1, 1))


def lanes_of(shape):
    return lax.broadcasted_iota(jnp.int32, shape, len(shape) - 1)


def turn(x, by, axis):
    return pltpu.roll(x, by % x.shape[axis], axis)


def ring_next(x):
    turned = turn(x, -1, 2)
    after = jnp.concatenate([turned[1:], turned[:1]], axis=0)
    return jnp.where(lanes_of(x.shape) == LANES - 1, after, turned)


def ring_previous(x):
    turned = turn(x, 1, 2)
    before = jnp.concatenate([turned[-1:], turned[:-1]], axis=0)
    return jnp.where(lanes_of(x.shape) == 0, before, turned)


def by_group(function, group, arrays):
    count = arrays[0].shape[0]
    pieces = [function(*(x[at : at + group] for x in arrays)) for at in range(0, count, group)]
    return [jnp.concatenate(column, axis=0) for column in zip(*pieces)]


def fluxes(h, p, q):
    floored = jnp.maximum(h, DRY_DEPTH)
    inverse_root = lax.rsqrt(floored)
    celerity = floored * (SCALE * inverse_root)
    inverse = inverse_root * inverse_root
    u = p * inverse
    v = q * inverse
    pressure = (0.5 * SCALE * SCALE) * h * h
    east, cross, north = p * u + pressure, q * u, q * v + pressure
    speed = jnp.abs(u) + celerity
    turned = tuple(turn(x, -1, 2) for x in (h, p, q, east, cross, speed))
    return (east, cross, speed, north, jnp.abs(v) + celerity) + turned


def faces(h, p, q, flux_h, flux_p, flux_q, speed, h_on, p_on, q_on, flux_h_on, flux_p_on, flux_q_on, speed_on):
    wave = jnp.maximum(speed, speed_on)
    return (
        flux_h + flux_h_on - wave * (h_on - h),
        flux_p + flux_p_on - wave * (p_on - p),
        flux_q + flux_q_on - wave * (q_on - q),
    )


def column_faces(h, p, q, east, cross, speed, *turned):
    count = h.shape[0]
    last = lanes_of(h.shape) == LANES - 1
    h_on, p_on, q_on, east_on, cross_on, speed_on = (
        jnp.where(last, after, x) for x, after in zip(turned[:6], turned[6:])
    )
    values = faces(h, p, q, p, east, cross, speed, h_on, p_on, q_on, p_on, east_on, cross_on, speed_on)
    return values + tuple(turn(x, 1, 2) for x in values)


def update(h, p, q, cross, north, speed, *rest):
    columns, slopes, mask, start = rest[:9], rest[9:11], rest[11], rest[12:]
    hb, pb, qb, cross_b, north_b, speed_b = (turn(x, -1, 1) for x in (h, p, q, cross, north, speed))
    rows = faces(h, p, q, q, cross, north, speed, hb, pb, qb, qb, cross_b, north_b, speed_b)
    first = lanes_of(h.shape) == 0
    moved = []
    for f, cells in enumerate((h, p, q)):
        face, back, before = columns[f::3]
        new = cells - ((face - jnp.where(first, before, back)) + (rows[f] - turn(rows[f], 1, 1)))
        if f:
            new = new - h * slopes[f - 1]
        if start:
            new = 0.5 * (start[f] + new)
        moved.append(new * mask)
    return moved


def half_step(state, slopes, masks, start):
    h, p, q = state
    group = GROUP if h.shape[1] > 2 * ROWS else GROUP_2
    east, cross, reach_x, north, reach_y, *turned = by_group(fluxes, group, state)
    here = [h, p, q, east, cross, reach_x]
    after = [jnp.concatenate([x[1:], x[:1]], axis=0) for x in turned]
    columns = by_group(column_faces, group, here + turned + after)
    before = [jnp.concatenate([x[-1:], x[:-1]], axis=0) for x in columns[3:]]
    others = columns + before + list(slopes) + [masks] + list(start or ())
    return by_group(update, group, [h, p, q, cross, north, reach_y] + others)


def two_steps(state, slopes, masks):
    for _ in range(2):
        middle = half_step(state, slopes, masks, None)
        state = half_step(middle, slopes, masks, state)
    return state


def kernel(
    sizes,
    depth_hbm,
    velocity_hbm,
    bed_hbm,
    wet_hbm,
    migration_hbm,
    out_ref,
    own,
    above,
    below,
    strip,
    strips,
    corners,
    wet,
    migration,
    tiles,
    outgoing,
    arrived,
    load_sem,
    halo_send,
    halo_recv,
    strip_send,
    strip_recv,
    corner_send,
    corner_recv,
    slot_send,
    slot_recv,
    lower,
    higher,
):
    n_rows, n_cols = sizes
    tile_count = own.shape[2] // LANES
    gx, gy = lax.axis_index("gx"), lax.axis_index("gy")
    has_up, has_down, has_left, has_right = gx > 0, gx < n_rows - 1, gy > 0, gy < n_cols - 1
    up, down = lax.rem(gx + n_rows - 1, n_rows), lax.rem(gx + 1, n_rows)
    left, right = lax.rem(gy + n_cols - 1, n_cols), lax.rem(gy + 1, n_cols)
    corner_ids = [((up, down)[r], (left, right)[s]) for r, s in CORNERS]
    has_corner = [(has_up, has_down)[r] & (has_left, has_right)[s] for r, s in CORNERS]

    def remote(source, target, send, receive, where):
        return pltpu.make_async_remote_copy(
            src_ref=source, dst_ref=target, send_sem=send, recv_sem=receive, device_id=where, device_id_type=MESH
        )

    barrier = pltpu.get_barrier_semaphore()

    def greet(friend):
        pl.semaphore_signal(barrier, inc=1, device_id=friend, device_id_type=MESH)

    beyond = [(has_up, (up, gy)), (has_down, (down, gy)), (has_left, (gx, left)), (has_right, (gx, right))]
    beyond += list(zip(has_corner, corner_ids))

    for there, friend in beyond:
        pl.when(there)(functools.partial(greet, friend))
    friends = sum(there.astype(jnp.int32) for there, _ in beyond)

    loads = [
        pltpu.make_async_copy(depth_hbm, own.at[0], load_sem.at[0]),
        pltpu.make_async_copy(velocity_hbm, own.at[pl.ds(1, 2)], load_sem.at[1]),
        pltpu.make_async_copy(bed_hbm, own.at[3], load_sem.at[2]),
        pltpu.make_async_copy(wet_hbm, wet, load_sem.at[3]),
        pltpu.make_async_copy(migration_hbm, migration, load_sem.at[4]),
    ]
    for load in loads:
        load.start()
    for load in loads[:3]:
        load.wait()

    pl.semaphore_wait(barrier, friends)

    def each(copies, what):
        for copy in copies:
            getattr(copy, what)()

    ways = [(has_up, (up, gy), below), (has_down, (down, gy), above), (has_left, (gx, left), None), (has_right, (gx, right), None)]
    halos = []
    for i, (there, where, target) in enumerate(ways):
        copies = []
        if target is not None:
            copies.append(remote(own, target, halo_send.at[i], halo_recv.at[i], where))
            pl.when(there)(functools.partial(each, copies, "start"))
        halos.append((there, copies))

    for load in loads[3:]:
        load.wait()

    lane = lanes_of((ROWS, LANES))
    packed = jnp.zeros((ROWS, LANES), jnp.float32)
    for f in range(4):
        first, last = own[f, :, 0:LANES], own[f, :, (tile_count - 1) * LANES : tile_count * LANES]
        at = REACH * f
        packed = jnp.where((lane >= at) & (lane < at + REACH), turn(first, at, 1) if f else first, packed)
        at = LANES - REACH * (f + 1)
        packed = jnp.where((lane >= at) & (lane < at + REACH), turn(last, -REACH * f, 1) if f else last, packed)
    for t in range(tile_count):
        packed = jnp.where(lane == WET_LANE + t, wet[0, t].astype(jnp.float32), packed)
    strip[...] = packed

    for i, (there, where, _) in enumerate(ways):
        copy = remote(strip, strips.at[i], strip_send.at[i], strip_recv.at[i], where)
        pl.when(there)(copy.start)
        halos[i][1].append(copy)
    for i, (there, where) in enumerate(zip(has_corner, corner_ids)):
        copy = remote(strip, corners.at[i], corner_send.at[i], corner_recv.at[i], where)
        pl.when(there)(copy.start)
        halos.append((there, [copy]))
    opposite = [1, 0, 3, 2, 7, 6, 5, 4]
    @pl.when(has_left)
    def _():
        pl.semaphore_wait(lower, 1)

    @pl.when(has_right)
    def _():
        pl.semaphore_signal(lower, inc=1, device_id=(gx, right), device_id_type=MESH)

    def announce(target, carry):
        pl.semaphore_signal(higher, inc=1, device_id=(gx, target), device_id_type=MESH)
        return carry

    lax.fori_loop(0, gy, announce, 0)

    chosen = []
    for target in range(n_cols):
        index = jnp.int32(-1)
        for t in range(tile_count):
            index = jnp.where(migration[0, t] == target, t, index)
        chosen.append(index)

    for (there, _), i in zip(halos, opposite):
        pl.when(there)(functools.partial(each, halos[i][1], "wait_recv"))

    def columns(reference, f):
        return [reference[f, :, c * LANES : (c + 1) * LANES] for c in range(tile_count)]

    def ends(from_left, from_right, f):
        head = turn(from_right, -REACH * f, 1) if f else from_right
        tail = turn(from_left, REACH * f, 1) if f else from_left
        return jnp.where(lane < REACH, head, jnp.where(lane >= LANES - REACH, tail, 0.0))

    lower_right, upper_right, lower_left, upper_left = (corners[i] for i in range(4))
    bands = (
        (above, upper_left, upper_right, strips[1]),
        (own, strips[3], strips[2], strip[...]),
        (below, lower_left, lower_right, strips[0]),
    )
    fields = []
    for f in range(4):
        stacked = [columns(band[0], f) + [ends(band[1], band[2], f)] for band in bands]
        fields.append([jnp.concatenate([s[c] for s in stacked], axis=0) for c in range(tile_count + 1)])

    def spread(tile, at):
        return jnp.broadcast_to(tile[:, at : at + 1], (ROWS, LANES))

    wets = []
    for c in range(tile_count + 1):
        stacked = []
        for _, from_left, from_right, flags in bands:
            if c < tile_count:
                stacked.append(spread(flags, WET_LANE + c))
            else:
                stacked.append(
                    jnp.where(
                        lane < LANES // 2, spread(from_right, WET_LANE), spread(from_left, WET_LANE + tile_count - 1)
                    )
                )
        wets.append(jnp.concatenate(stacked, axis=0))

    row = lax.broadcasted_iota(jnp.int32, (3 * ROWS, LANES), 0)
    wide = lanes_of((3 * ROWS, LANES))
    weights = [there.astype(jnp.float32) for there in (has_up, has_down, has_left, has_right)]
    inside_rows = jnp.where(row < ROWS, weights[0], jnp.where(row >= 2 * ROWS, weights[1], jnp.float32(1)))
    inside_ends = inside_rows * jnp.where(wide < LANES // 2, weights[3], weights[2])
    masks = [inside_rows] * tile_count + [inside_ends]

    masks = jnp.stack(masks)
    depth, across, along, beds = (jnp.where(masks > 0.5, jnp.stack(field), 0.0) for field in fields)
    scaled = SCALE * depth
    state = (depth, scaled * across, scaled * along)
    slopes = (
        (SCALE * SCALE) * (ring_next(beds) - ring_previous(beds)),
        (SCALE * SCALE) * (turn(beds, -1, 1) - turn(beds, 1, 1)),
    )
    wets = jnp.stack(wets)
    advanced = two_steps(state, slopes, masks)
    state = tuple(jnp.where(wets > 0.5, new, old) for new, old in zip(advanced, state))

    def narrow(x, start, size):
        return turn(x, -start, 1)[:, :size]

    kept = 2 * HALO + ROWS
    state = tuple(narrow(x, ROWS - HALO, kept) for x in state)
    slopes = tuple(narrow(x, ROWS - HALO, kept) for x in slopes)
    advanced = two_steps(state, slopes, narrow(masks, ROWS - HALO, kept))
    wet = wets[:tile_count, ROWS : 2 * ROWS] > 0.5
    for f in range(3):
        new, old = narrow(advanced[f], HALO, ROWS)[:tile_count], narrow(state[f], HALO, ROWS)[:tile_count]
        tiles[:, f * ROWS : (f + 1) * ROWS] = jnp.where(wet, new, old) * (1.0 / SCALE if f else 1.0)

    for target in range(n_cols):
        outgoing[target, : 3 * ROWS] = tiles[jnp.maximum(chosen[target], 0)]
        outgoing[target, TAG : TAG + 1] = jnp.full((1, LANES), chosen[target].astype(jnp.float32))
    arrived[gy] = outgoing[gy]

    slot = pl.ds(0, TAG + 1)

    def send_slot(target, carry):
        remote(outgoing.at[target, slot], arrived.at[gy, slot], slot_send, slot_recv, (gx, target)).start()
        return carry

    def from_both_ends(i, carry):
        half = i // 2
        return send_slot(jnp.where(lax.rem(i, 2) == 0, half, gy - 1 - half), carry)

    lax.fori_loop(0, gy, from_both_ends, 0)

    @pl.when(has_right)
    def _():
        pl.semaphore_wait(higher, n_cols - 1 - gy)

    lax.fori_loop(gy + 1, n_cols, send_slot, 0)

    others = pl.ds(0, n_cols - 1)
    all_slots = remote(outgoing.at[others, slot], arrived.at[others, slot], slot_send, slot_recv, (gx, right))
    all_slots.wait_recv()
    placed = [[jnp.zeros((ROWS, LANES), jnp.float32) for _ in range(3)] for _ in range(tile_count)]
    for source in range(n_cols):
        tag = jnp.broadcast_to(arrived[source, TAG : TAG + 1], (ROWS, LANES))
        cells = [arrived[source, f * ROWS : (f + 1) * ROWS] for f in range(3)]
        for t in range(tile_count):
            here = tag == jnp.float32(t)
            placed[t] = [jnp.where(here, new, old) for new, old in zip(cells, placed[t])]
    for t in range(tile_count):
        for f in range(3):
            out_ref[f, :, t * LANES : (t + 1) * LANES] = placed[t][f]
    for there, copies in halos:
        pl.when(there)(functools.partial(each, copies, "wait_send"))
    all_slots.wait_send()


def solution(mesh):
    n_rows, n_cols = mesh.shape["gx"], mesh.shape["gy"]

    def step(water_depth, velocity, bathymetry, wet_tiles, migration):
        rows, cols = water_depth.shape
        tile_count = wet_tiles.shape[1]
        block = (4, rows, cols)
        dma = pltpu.SemaphoreType.DMA
        return pl.pallas_call(
            functools.partial(kernel, (n_rows, n_cols)),
            out_shape=pltpu.VMEM((3, rows, cols), jnp.float32),
            in_specs=[pl.BlockSpec(memory_space=pl.ANY)] * 5,
            out_specs=pl.BlockSpec(memory_space=pltpu.VMEM),
            scratch_shapes=[
                pltpu.VMEM(block, jnp.float32),
                pltpu.VMEM(block, jnp.float32),
                pltpu.VMEM(block, jnp.float32),
                pltpu.VMEM((ROWS, LANES), jnp.float32),
                pltpu.VMEM((4, ROWS, LANES), jnp.float32),
                pltpu.VMEM((4, ROWS, LANES), jnp.float32),
                pltpu.SMEM((1, tile_count), jnp.int32),
                pltpu.SMEM((1, tile_count), jnp.int32),
                pltpu.VMEM((tile_count, 3 * rows, LANES), jnp.float32),
                pltpu.VMEM((n_cols, 4 * rows, LANES), jnp.float32),
                pltpu.VMEM((n_cols, 4 * rows, LANES), jnp.float32),
                dma((5,)),
                dma((2,)),
                dma((2,)),
                dma((4,)),
                dma((4,)),
                dma((4,)),
                dma((4,)),
                dma,
                dma,
                pltpu.SemaphoreType.REGULAR,
                pltpu.SemaphoreType.REGULAR,
            ],
            compiler_params=pltpu.CompilerParams(
                collective_id=0, has_side_effects=True, vmem_limit_bytes=32 * 1024 * 1024
            ),
        )(*(pltpu.with_memory_space_constraint(x, pltpu.HBM) for x in (water_depth, velocity, bathymetry, wet_tiles, migration)))

    return jax.shard_map(
        step,
        mesh=mesh,
        in_specs=(P("gx", "gy"), P(None, "gx", "gy"), P("gx", "gy"), P("gx", "gy"), P("gx", "gy")),
        out_specs=P(None, "gx", "gy"),
        check_vma=False,
    )
```

```python
import functools

import jax
import jax.numpy as jnp
from jax import lax
from jax.experimental import pallas as pl
from jax.experimental.pallas import tpu as pltpu
from jax.sharding import PartitionSpec as P

DRY_DEPTH = 0.05
COURANT = 0.15
SCALE = 0.5 * COURANT
HALO = 4
ROWS = 8
LANES = 128
TAG = 3 * ROWS
GROUP, GROUP_2 = 2, 2
REACH = 8
WET_LANE = 32
MESH = pl.DeviceIdType.MESH
CORNERS = ((0, 0), (1, 0), (0, 1), (1, 1))


def lanes_of(shape):
    return lax.broadcasted_iota(jnp.int32, shape, len(shape) - 1)


def turn(x, by, axis):
    return pltpu.roll(x, by % x.shape[axis], axis)


def ring_next(x):
    turned = turn(x, -1, 2)
    after = jnp.concatenate([turned[1:], turned[:1]], axis=0)
    return jnp.where(lanes_of(x.shape) == LANES - 1, after, turned)


def ring_previous(x):
    turned = turn(x, 1, 2)
    before = jnp.concatenate([turned[-1:], turned[:-1]], axis=0)
    return jnp.where(lanes_of(x.shape) == 0, before, turned)


def by_group(function, group, arrays):
    count = arrays[0].shape[0]
    pieces = [function(*(x[at : at + group] for x in arrays)) for at in range(0, count, group)]
    return [jnp.concatenate(column, axis=0) for column in zip(*pieces)]


def fluxes(h, p, q):
    floored = jnp.maximum(h, DRY_DEPTH)
    inverse_root = lax.rsqrt(floored)
    celerity = floored * (SCALE * inverse_root)
    inverse = inverse_root * inverse_root
    u = p * inverse
    v = q * inverse
    pressure = (0.5 * SCALE * SCALE) * h * h
    east, cross, north = p * u + pressure, q * u, q * v + pressure
    speed = jnp.abs(u) + celerity
    turned = tuple(turn(x, -1, 2) for x in (h, p, q, east, cross, speed))
    return (east, cross, speed, north, jnp.abs(v) + celerity) + turned


def faces(h, p, q, flux_h, flux_p, flux_q, speed, h_on, p_on, q_on, flux_h_on, flux_p_on, flux_q_on, speed_on):
    wave = jnp.maximum(speed, speed_on)
    return (
        flux_h + flux_h_on - wave * (h_on - h),
        flux_p + flux_p_on - wave * (p_on - p),
        flux_q + flux_q_on - wave * (q_on - q),
    )


def column_faces(h, p, q, east, cross, speed, *turned):
    count = h.shape[0]
    last = lanes_of(h.shape) == LANES - 1
    h_on, p_on, q_on, east_on, cross_on, speed_on = (
        jnp.where(last, after, x) for x, after in zip(turned[:6], turned[6:])
    )
    values = faces(h, p, q, p, east, cross, speed, h_on, p_on, q_on, p_on, east_on, cross_on, speed_on)
    return values + tuple(turn(x, 1, 2) for x in values)


def update(h, p, q, cross, north, speed, *rest):
    columns, slopes, mask, start = rest[:9], rest[9:11], rest[11], rest[12:]
    hb, pb, qb, cross_b, north_b, speed_b = (turn(x, -1, 1) for x in (h, p, q, cross, north, speed))
    rows = faces(h, p, q, q, cross, north, speed, hb, pb, qb, qb, cross_b, north_b, speed_b)
    first = lanes_of(h.shape) == 0
    moved = []
    for f, cells in enumerate((h, p, q)):
        face, back, before = columns[f::3]
        new = cells - ((face - jnp.where(first, before, back)) + (rows[f] - turn(rows[f], 1, 1)))
        if f:
            new = new - h * slopes[f - 1]
        if start:
            new = 0.5 * (start[f] + new)
        moved.append(new * mask)
    return moved


def half_step(state, slopes, masks, start, kept=None):
    h, p, q = state
    group = GROUP if h.shape[1] > 2 * ROWS else GROUP_2
    east, cross, reach_x, north, reach_y, *turned = by_group(fluxes, group, state)
    here = [h, p, q, east, cross, reach_x]
    after = [jnp.concatenate([x[1:], x[:1]], axis=0) for x in turned]
    columns = by_group(column_faces, group, here + turned + after)
    before = [jnp.concatenate([x[-1:], x[:-1]], axis=0) for x in columns[3:]]
    others = columns + before + list(slopes) + [masks] + list(start or ())
    return by_group(update, group, [x[:kept] for x in [h, p, q, cross, north, reach_y] + others])


def two_steps(state, slopes, masks, kept=None):
    for step in range(2):
        middle = half_step(state, slopes, masks, None)
        state = half_step(middle, slopes, masks, state, kept if step else None)
    return state


def kernel(
    sizes,
    depth_hbm,
    velocity_hbm,
    bed_hbm,
    wet_hbm,
    migration_hbm,
    out_ref,
    own,
    above,
    below,
    strip,
    strips,
    corners,
    wet,
    migration,
    tiles,
    outgoing,
    arrived,
    load_sem,
    halo_send,
    halo_recv,
    strip_send,
    strip_recv,
    corner_send,
    corner_recv,
    slot_send,
    slot_recv,
    lower,
    higher,
):
    n_rows, n_cols = sizes
    tile_count = own.shape[2] // LANES
    gx, gy = lax.axis_index("gx"), lax.axis_index("gy")
    has_up, has_down, has_left, has_right = gx > 0, gx < n_rows - 1, gy > 0, gy < n_cols - 1
    up, down = lax.rem(gx + n_rows - 1, n_rows), lax.rem(gx + 1, n_rows)
    left, right = lax.rem(gy + n_cols - 1, n_cols), lax.rem(gy + 1, n_cols)
    corner_ids = [((up, down)[r], (left, right)[s]) for r, s in CORNERS]
    has_corner = [(has_up, has_down)[r] & (has_left, has_right)[s] for r, s in CORNERS]

    def remote(source, target, send, receive, where):
        return pltpu.make_async_remote_copy(
            src_ref=source, dst_ref=target, send_sem=send, recv_sem=receive, device_id=where, device_id_type=MESH
        )

    barrier = pltpu.get_barrier_semaphore()

    def greet(friend):
        pl.semaphore_signal(barrier, inc=1, device_id=friend, device_id_type=MESH)

    beyond = [(has_up, (up, gy)), (has_down, (down, gy)), (has_left, (gx, left)), (has_right, (gx, right))]
    beyond += list(zip(has_corner, corner_ids))

    for there, friend in beyond:
        pl.when(there)(functools.partial(greet, friend))
    friends = sum(there.astype(jnp.int32) for there, _ in beyond)

    loads = [
        pltpu.make_async_copy(depth_hbm, own.at[0], load_sem.at[0]),
        pltpu.make_async_copy(velocity_hbm, own.at[pl.ds(1, 2)], load_sem.at[1]),
        pltpu.make_async_copy(bed_hbm, own.at[3], load_sem.at[2]),
        pltpu.make_async_copy(wet_hbm, wet, load_sem.at[3]),
        pltpu.make_async_copy(migration_hbm, migration, load_sem.at[4]),
    ]
    for load in loads:
        load.start()
    for load in loads[:3]:
        load.wait()

    pl.semaphore_wait(barrier, friends)

    def each(copies, what):
        for copy in copies:
            getattr(copy, what)()

    ways = [(has_up, (up, gy), below), (has_down, (down, gy), above), (has_left, (gx, left), None), (has_right, (gx, right), None)]
    halos = []
    for i, (there, where, target) in enumerate(ways):
        copies = []
        if target is not None:
            copies.append(remote(own, target, halo_send.at[i], halo_recv.at[i], where))
            pl.when(there)(functools.partial(each, copies, "start"))
        halos.append((there, copies))

    for load in loads[3:]:
        load.wait()

    lane = lanes_of((ROWS, LANES))
    packed = jnp.zeros((ROWS, LANES), jnp.float32)
    for f in range(4):
        first, last = own[f, :, 0:LANES], own[f, :, (tile_count - 1) * LANES : tile_count * LANES]
        at = REACH * f
        packed = jnp.where((lane >= at) & (lane < at + REACH), turn(first, at, 1) if f else first, packed)
        at = LANES - REACH * (f + 1)
        packed = jnp.where((lane >= at) & (lane < at + REACH), turn(last, -REACH * f, 1) if f else last, packed)
    for t in range(tile_count):
        packed = jnp.where(lane == WET_LANE + t, wet[0, t].astype(jnp.float32), packed)
    strip[...] = packed

    for i, (there, where, _) in enumerate(ways):
        copy = remote(strip, strips.at[i], strip_send.at[i], strip_recv.at[i], where)
        pl.when(there)(copy.start)
        halos[i][1].append(copy)
    for i, (there, where) in enumerate(zip(has_corner, corner_ids)):
        copy = remote(strip, corners.at[i], corner_send.at[i], corner_recv.at[i], where)
        pl.when(there)(copy.start)
        halos.append((there, [copy]))
    opposite = [1, 0, 3, 2, 7, 6, 5, 4]
    @pl.when(has_left)
    def _():
        pl.semaphore_wait(lower, 1)

    @pl.when(has_right)
    def _():
        pl.semaphore_signal(lower, inc=1, device_id=(gx, right), device_id_type=MESH)

    def announce(target, carry):
        pl.semaphore_signal(higher, inc=1, device_id=(gx, target), device_id_type=MESH)
        return carry

    lax.fori_loop(0, gy, announce, 0)

    chosen = []
    for target in range(n_cols):
        index = jnp.int32(-1)
        for t in range(tile_count):
            index = jnp.where(migration[0, t] == target, t, index)
        chosen.append(index)

    for (there, _), i in zip(halos, opposite):
        pl.when(there)(functools.partial(each, halos[i][1], "wait_recv"))

    def columns(reference, f):
        return [reference[f, :, c * LANES : (c + 1) * LANES] for c in range(tile_count)]

    def ends(from_left, from_right, f):
        head = turn(from_right, -REACH * f, 1) if f else from_right
        tail = turn(from_left, REACH * f, 1) if f else from_left
        return jnp.where(lane < REACH, head, jnp.where(lane >= LANES - REACH, tail, 0.0))

    lower_right, upper_right, lower_left, upper_left = (corners[i] for i in range(4))
    bands = (
        (above, upper_left, upper_right, strips[1]),
        (own, strips[3], strips[2], strip[...]),
        (below, lower_left, lower_right, strips[0]),
    )
    fields = []
    for f in range(4):
        stacked = [columns(band[0], f) + [ends(band[1], band[2], f)] for band in bands]
        fields.append([jnp.concatenate([s[c] for s in stacked], axis=0) for c in range(tile_count + 1)])

    def spread(tile, at):
        return jnp.broadcast_to(tile[:, at : at + 1], (ROWS, LANES))

    wets = []
    for c in range(tile_count + 1):
        stacked = []
        for _, from_left, from_right, flags in bands:
            if c < tile_count:
                stacked.append(spread(flags, WET_LANE + c))
            else:
                stacked.append(
                    jnp.where(
                        lane < LANES // 2, spread(from_right, WET_LANE), spread(from_left, WET_LANE + tile_count - 1)
                    )
                )
        wets.append(jnp.concatenate(stacked, axis=0))

    row = lax.broadcasted_iota(jnp.int32, (3 * ROWS, LANES), 0)
    wide = lanes_of((3 * ROWS, LANES))
    weights = [there.astype(jnp.float32) for there in (has_up, has_down, has_left, has_right)]
    inside_rows = jnp.where(row < ROWS, weights[0], jnp.where(row >= 2 * ROWS, weights[1], jnp.float32(1)))
    inside_ends = inside_rows * jnp.where(wide < LANES // 2, weights[3], weights[2])
    masks = [inside_rows] * tile_count + [inside_ends]

    masks = jnp.stack(masks)
    depth, across, along, beds = (jnp.where(masks > 0.5, jnp.stack(field), 0.0) for field in fields)
    scaled = SCALE * depth
    state = (depth, scaled * across, scaled * along)
    slopes = (
        (SCALE * SCALE) * (ring_next(beds) - ring_previous(beds)),
        (SCALE * SCALE) * (turn(beds, -1, 1) - turn(beds, 1, 1)),
    )
    wets = jnp.stack(wets)
    advanced = two_steps(state, slopes, masks)
    state = tuple(jnp.where(wets > 0.5, new, old) for new, old in zip(advanced, state))

    def narrow(x, start, size):
        return turn(x, -start, 1)[:, :size]

    kept = 2 * HALO + ROWS
    state = tuple(narrow(x, ROWS - HALO, kept) for x in state)
    slopes = tuple(narrow(x, ROWS - HALO, kept) for x in slopes)
    advanced = two_steps(state, slopes, narrow(masks, ROWS - HALO, kept), tile_count)
    wet = wets[:tile_count, ROWS : 2 * ROWS] > 0.5
    for f in range(3):
        new, old = narrow(advanced[f], HALO, ROWS)[:tile_count], narrow(state[f], HALO, ROWS)[:tile_count]
        tiles[:, f * ROWS : (f + 1) * ROWS] = jnp.where(wet, new, old) * (1.0 / SCALE if f else 1.0)

    for target in range(n_cols):
        outgoing[target, : 3 * ROWS] = tiles[jnp.maximum(chosen[target], 0)]
        outgoing[target, TAG : TAG + 1] = jnp.full((1, LANES), chosen[target].astype(jnp.float32))
    arrived[gy] = outgoing[gy]

    slot = pl.ds(0, TAG + 1)

    def send_slot(target, carry):
        remote(outgoing.at[target, slot], arrived.at[gy, slot], slot_send, slot_recv, (gx, target)).start()
        return carry

    def from_both_ends(i, carry):
        half = i // 2
        return send_slot(jnp.where(lax.rem(i, 2) == 0, half, gy - 1 - half), carry)

    lax.fori_loop(0, gy, from_both_ends, 0)

    @pl.when(has_right)
    def _():
        pl.semaphore_wait(higher, n_cols - 1 - gy)

    lax.fori_loop(gy + 1, n_cols, send_slot, 0)

    others = pl.ds(0, n_cols - 1)
    all_slots = remote(outgoing.at[others, slot], arrived.at[others, slot], slot_send, slot_recv, (gx, right))
    all_slots.wait_recv()
    placed = [[jnp.zeros((ROWS, LANES), jnp.float32) for _ in range(3)] for _ in range(tile_count)]
    for source in range(n_cols):
        tag = jnp.broadcast_to(arrived[source, TAG : TAG + 1], (ROWS, LANES))
        cells = [arrived[source, f * ROWS : (f + 1) * ROWS] for f in range(3)]
        for t in range(tile_count):
            here = tag == jnp.float32(t)
            placed[t] = [jnp.where(here, new, old) for new, old in zip(cells, placed[t])]
    for t in range(tile_count):
        for f in range(3):
            out_ref[f, :, t * LANES : (t + 1) * LANES] = placed[t][f]
    for there, copies in halos:
        pl.when(there)(functools.partial(each, copies, "wait_send"))
    all_slots.wait_send()


def solution(mesh):
    n_rows, n_cols = mesh.shape["gx"], mesh.shape["gy"]

    def step(water_depth, velocity, bathymetry, wet_tiles, migration):
        rows, cols = water_depth.shape
        tile_count = wet_tiles.shape[1]
        block = (4, rows, cols)
        dma = pltpu.SemaphoreType.DMA
        return pl.pallas_call(
            functools.partial(kernel, (n_rows, n_cols)),
            out_shape=pltpu.VMEM((3, rows, cols), jnp.float32),
            in_specs=[pl.BlockSpec(memory_space=pl.ANY)] * 5,
            out_specs=pl.BlockSpec(memory_space=pltpu.VMEM),
            scratch_shapes=[
                pltpu.VMEM(block, jnp.float32),
                pltpu.VMEM(block, jnp.float32),
                pltpu.VMEM(block, jnp.float32),
                pltpu.VMEM((ROWS, LANES), jnp.float32),
                pltpu.VMEM((4, ROWS, LANES), jnp.float32),
                pltpu.VMEM((4, ROWS, LANES), jnp.float32),
                pltpu.SMEM((1, tile_count), jnp.int32),
                pltpu.SMEM((1, tile_count), jnp.int32),
                pltpu.VMEM((tile_count, 3 * rows, LANES), jnp.float32),
                pltpu.VMEM((n_cols, 4 * rows, LANES), jnp.float32),
                pltpu.VMEM((n_cols, 4 * rows, LANES), jnp.float32),
                dma((5,)),
                dma((2,)),
                dma((2,)),
                dma((4,)),
                dma((4,)),
                dma((4,)),
                dma((4,)),
                dma,
                dma,
                pltpu.SemaphoreType.REGULAR,
                pltpu.SemaphoreType.REGULAR,
            ],
            compiler_params=pltpu.CompilerParams(
                collective_id=0, has_side_effects=True, vmem_limit_bytes=32 * 1024 * 1024
            ),
        )(*(pltpu.with_memory_space_constraint(x, pltpu.HBM) for x in (water_depth, velocity, bathymetry, wet_tiles, migration)))

    return jax.shard_map(
        step,
        mesh=mesh,
        in_specs=(P("gx", "gy"), P(None, "gx", "gy"), P("gx", "gy"), P("gx", "gy"), P("gx", "gy")),
        out_specs=P(None, "gx", "gy"),
        check_vma=False,
    )
```
